32 devices in a mesh: dp: 32 (over z, y, x, core).
Axes of the slice: x: 2, y: 2, z: 4, core: 2. Of those that a mesh axis runs over, the one named last changes fastest.
Arguments:
- tokens: bfloat16 [32768, 768], P('dp'), may hold values from -12 to 12
- cotangent: bfloat16 [32768, 768], P('dp'), may hold values from -12 to 12
- lengths: int32 [32, 8], P('dp'), may hold values from 0 to 512, as said below
- w_qkv: bfloat16 [768, 2304], P('dp'), may hold values from -0.21875 to 0.21875
- w_out: bfloat16 [768, 768], P('dp'), may hold values from -0.875 to 0.875
- w_up: bfloat16 [768, 3072], P('dp'), may hold values from -0.21875 to 0.21875
- w_down: bfloat16 [3072, 768], P('dp'), may hold values from -0.109375 to 0.109375
- bias_q: bfloat16 [768], P('dp'), may hold values from -1.75 to 1.75
- bias_v: bfloat16 [768], P('dp'), may hold values from -1.75 to 1.75
- bias_out: bfloat16 [768], P('dp'), may hold values from -1.75 to 1.75
- gain_one: bfloat16 [768], P('dp'), may hold values from 0.5 to 1.5
- shift_one: bfloat16 [768], P('dp'), may hold values from -1.75 to 1.75
- bias_up: bfloat16 [3072], P('dp'), may hold values from -3 to 3
- bias_down: bfloat16 [768], P('dp'), may hold values from -1.75 to 1.75
- gain_two: bfloat16 [768], P('dp'), may hold values from 0.5 to 1.5
- shift_two: bfloat16 [768], P('dp'), may hold values from -1.75 to 1.75
Outputs:
- output: bfloat16 [32768, 768], P('dp')
- grad_tokens: float32 [32768, 768], P('dp')
- grad_w_qkv: float32 [768, 2304], P('dp')
- grad_w_out: float32 [768, 768], P('dp')
- grad_w_up: float32 [768, 3072], P('dp')
- grad_w_down: float32 [3072, 768], P('dp')
- grad_bias_q: float32 [768], P('dp')
- grad_bias_v: float32 [768], P('dp')
- grad_bias_out: float32 [768], P('dp')
- grad_gain_one: float32 [768], P('dp')
- grad_shift_one: float32 [768], P('dp')
- grad_bias_up: float32 [3072], P('dp')
- grad_bias_down: float32 [768], P('dp')
- grad_gain_two: float32 [768], P('dp')
- grad_shift_two: float32 [768], P('dp')
The draws below stay inside these ranges and needn't reach their ends.
Inputs may be any that keep to these rules, and one draw needn't show every extreme that they name: Row d lists the lengths of the sequences packed on device d, laid end to end from its first row and followed by padding; its nonzero entries come first and are 128 or more, and they sum to at most 1024; some device holds exactly 2 sequences of 512 tokens.
All inputs are finite; a program needn't handle non-finite values.
Results may differ from the reference program's by a relative error of at most 0.014.
Values may be sent and summed in bfloat16 or wider, within the bound.
No kernel may reach another device: no remote copies, remote signals or barrier semaphores. Data moves between devices by JAX's collectives and lax.ppermute only.
A program may use at most 192 MiB of HBM per device.

```python
import math
import jax
import jax.numpy as jnp
from jax import lax

D = 768
HD = 64
FF = 3072
MAXLEN = 512
TOK_DEV = 1024
SLOTS = 8
TOKENS = 32768
N_DP = 32


def draw_lengths(key, part):
    key = jax.random.fold_in(key, 11)
    key_len, key_full = jax.random.split(key)
    drawn = jax.random.randint(key_len, (N_DP, SLOTS), MAXLEN // 4, MAXLEN + 1)
    running = jnp.cumsum(drawn, axis=1)
    trimmed = jnp.where(running <= TOK_DEV, drawn, 0)
    chosen = jax.random.randint(key_full, (), 0, N_DP)
    column = jnp.arange(SLOTS)
    full_row = jnp.where(column < TOK_DEV // MAXLEN, MAXLEN, 0)
    device = jnp.arange(N_DP)
    return jnp.where((device == chosen)[:, None], full_row[None, :], trimmed).astype(jnp.int32)


def raised(entries, stream_key, source, target, blocks, factor):
    def block_of(dim):
        return (jnp.arange(entries.shape[dim]) // (entries.shape[dim] // blocks)).reshape((-1,) + (1,) * (entries.ndim - 1 - dim))

    near = jax.random.permutation(stream_key, blocks)[block_of(target)]
    other_side = (block_of(target) + blocks // 2) % blocks
    return jnp.where((block_of(source) == near) | (block_of(source) == other_side), factor * entries, entries)


def levels(key, dims, cuts, low, top_value):
    def one(dim, shards_of):
        steps = jax.random.uniform(jax.random.fold_in(jax.random.fold_in(key, 6), dim), (shards_of,), jnp.float32, low / len(cuts), top_value / len(cuts))
        return jnp.repeat(jnp.exp(steps), dims[dim] // shards_of).reshape((-1,) + (1,) * (len(dims) - dim - 1))

    factor_of = one(*cuts[0])
    for cut in cuts[1:]:
        factor_of = factor_of * one(*cut)
    return factor_of


def noise(stream_key, extent, deviation, most, cuts=(), kind=jnp.bfloat16):
    values = jax.random.normal(stream_key, extent, jnp.float32) * deviation
    if len(cuts) > 0:
        values = levels(stream_key, extent, cuts, -0.22, 0.18) * values
    return jnp.clip(values, min=-most, max=most).astype(kind)


def noise_with(stream_key, shape, scale, most, pieces, heavy, kind=jnp.bfloat16):
    values = scale * jax.random.normal(stream_key, shape, jnp.float32)
    if pieces:
        values = values * levels(stream_key, shape, pieces, -0.22, 0.18)
    return jnp.clip(raised(values, jax.random.fold_in(stream_key, 3), *heavy), -most, most).astype(kind)


def setup_inputs(seed: int = 0) -> dict:
    key_of = jax.random.split(jax.random.key(seed), 17)
    tokens = noise_with(key_of[0], (TOKENS, D), 1.0, 12.0, ((0, 32),), (0, 1, 32, 2.75))
    cotangent = noise_with(key_of[1], (TOKENS, D), 1.0, 12.0, ((0, 32),), (0, 1, 32, 2.75))
    lengths = draw_lengths(jax.random.fold_in(key_of[16], 71), 0)
    w_qkv = noise(key_of[3], (D, 3 * D), D ** -0.5, 0.21875, ((0, 32),))
    w_out = noise(key_of[4], (D, D), (D // 16) ** -0.5, 0.875, ((0, 32),))
    w_up = noise(key_of[5], (D, FF), D ** -0.5, 0.21875, ((0, 32),))
    w_down = noise(key_of[6], (FF, D), FF ** -0.5, 0.109375, ((0, 32),))
    bias_q = noise(key_of[7], (D,), 0.3, 1.75, ((0, 32),))
    bias_v = noise(key_of[8], (D,), 0.3, 1.75, ((0, 32),))
    bias_out = noise(key_of[9], (D,), 0.3, 1.75, ((0, 32),))
    gain_one = jnp.clip(1.0 + 0.1 * jax.random.normal(key_of[10], (D,), jnp.float32), 0.5, 1.5).astype(jnp.bfloat16)
    shift_one = noise(key_of[11], (D,), 0.3, 1.75, ((0, 32),))
    bias_up = noise(key_of[12], (FF,), 0.5, 3.0, ((0, 32),))
    bias_down = noise(key_of[13], (D,), 0.3, 1.75, ((0, 32),))
    gain_two = jnp.clip(1.0 + 0.1 * jax.random.normal(key_of[14], (D,), jnp.float32), 0.5, 1.5).astype(jnp.bfloat16)
    shift_two = noise(key_of[15], (D,), 0.3, 1.75, ((0, 32),))
    return {"tokens": tokens, "cotangent": cotangent, "lengths": lengths, "w_qkv": w_qkv, "w_out": w_out, "w_up": w_up, "w_down": w_down, "bias_q": bias_q, "bias_v": bias_v, "bias_out": bias_out, "gain_one": gain_one, "shift_one": shift_one, "bias_up": bias_up, "bias_down": bias_down, "gain_two": gain_two, "shift_two": shift_two}


@jax.custom_vjp
def low(v):
    return lax.optimization_barrier(v.astype(jnp.bfloat16)).astype(jnp.float32)

@jax.custom_vjp
def low_back(v):
    return v

def low_keep(v):
    return (low(v), None)

def low_pass(kept, grad):
    return (grad,)

def back_keep(v):
    return (v, None)

def back_low(kept, grad):
    return (low(grad),)
low.defvjp(low_keep, low_pass)
low_back.defvjp(back_keep, back_low)
norm_eps = 1e-06

def matmul(left, right):
    return jnp.dot(left, right, precision=lax.Precision.HIGHEST, preferred_element_type=jnp.float32)

def normalize(values, gain, shift):
    center = lax.optimization_barrier(jnp.mean(values, axis=-1, keepdims=True))
    centered = values - center
    spread = lax.optimization_barrier(jnp.mean(centered * centered, axis=-1, keepdims=True))
    return centered * lax.rsqrt(spread + norm_eps) * gain + shift

def segments(length_row, row_count):
    bounds = jnp.cumsum(length_row).astype(jnp.int32)
    position = jnp.arange(row_count, dtype=jnp.int32)
    member = lax.optimization_barrier(jnp.sum((position[:, None] >= bounds[None, :]).astype(jnp.int32), axis=1)).astype(jnp.int32)
    valid = position < bounds[-1]
    return (jnp.where(valid, member, position + length_row.shape[0]).astype(jnp.int32), valid)

def block_forward(x_rows, segment, valid, params):
    w_qkv, w_out, w_up, w_down, bias_q, bias_v, bias_out, gain_one, shift_one, bias_up, bias_down, gain_two, shift_two = params
    row_count = x_rows.shape[0]
    width = w_out.shape[0]
    head_count = width // HD
    scale_factor = 1.0 / math.sqrt(HD)
    query = low(low_back(matmul(x_rows, w_qkv[:, :width]) + bias_q))
    keys = low(low_back(matmul(x_rows, w_qkv[:, width:2 * width])))
    values = low(low_back(matmul(x_rows, w_qkv[:, 2 * width:]) + bias_v))
    query_h = query.reshape(row_count, head_count, HD)
    keys_h = keys.reshape(row_count, head_count, HD)
    values_h = values.reshape(row_count, head_count, HD)
    scores = jnp.einsum('qhd,khd->hqk', query_h, keys_h, precision=lax.Precision.HIGHEST) * scale_factor
    allowed = segment[:, None] == segment[None, :]
    scores = low_back(jnp.where(allowed[None], scores, -1000000000.0))
    probs = low(jax.nn.softmax(scores, axis=-1))
    mixed = jnp.einsum('hqk,khd->qhd', probs, values_h, precision=lax.Precision.HIGHEST).reshape(row_count, width)
    mixed = low(low_back(mixed))
    attn = low_back(matmul(mixed, w_out) + bias_out)
    hidden = normalize(x_rows + attn, gain_one, shift_one)
    up_pre = low_back(matmul(low(hidden), w_up) + bias_up)
    active = low(jax.nn.gelu(up_pre, approximate=False))
    branch = low_back(matmul(active, w_down) + bias_down)
    normed = normalize(hidden + branch, gain_two, shift_two)
    return jnp.where(valid[:, None], normed, 0.0)

def reference(tokens, cotangent, lengths, w_qkv, w_out, w_up, w_down, bias_q, bias_v, bias_out, gain_one, shift_one, bias_up, bias_down, gain_two, shift_two):
    params = tuple((array.astype(jnp.float32) for array in (w_qkv, w_out, w_up, w_down, bias_q, bias_v, bias_out, gain_one, shift_one, bias_up, bias_down, gain_two, shift_two)))

    def one_row(length_row):
        return segments(length_row, TOK_DEV)
    segment_all, valid_all = jax.vmap(one_row)(lengths)
    x_blocks = tokens.astype(jnp.float32).reshape(N_DP, TOK_DEV, D)
    cot_blocks = cotangent.astype(jnp.float32).reshape(N_DP, TOK_DEV, D)

    def forward(x_all, weights):

        def run_block(x_rows, segment, valid):
            return block_forward(x_rows, segment, valid, weights)
        checked = jax.checkpoint(run_block)

        def scan_body(carry, items):
            return (carry, checked(items[0], items[1], items[2]))
        _, result = lax.scan(scan_body, jnp.zeros((), jnp.float32), (x_all, segment_all, valid_all))
        return result
    result, pullback = jax.vjp(forward, x_blocks, params)
    grad_x, grads = pullback(cot_blocks)
    return (result.reshape(TOKENS, D).astype(jnp.bfloat16), grad_x.reshape(TOKENS, D), grads[0], grads[1], grads[2], grads[3], grads[4], grads[5], grads[6], grads[7], grads[8], grads[9], grads[10], grads[11], grads[12])
```

```python
import functools
import math

import jax
import jax.numpy as jnp
import numpy as np
from jax import lax
from jax.experimental import pallas as pl
from jax.experimental.pallas import tpu as pltpu
from jax.sharding import PartitionSpec as P

HD = 64
QB = 256
KB = 128
TB = 256
FB = 768
BLOCKS = 32
NORM_EPS = 1e-06
MASKED = -1000000000.0
SCALE = 1.0 / math.sqrt(HD)
NT = (((1,), (1,)), ((), ()))
TN = (((0,), (0,)), ((), ()))
f32 = jnp.float32
bf16 = jnp.bfloat16


def dot(a, b, dims=(((1,), (0,)), ((), ()))):
    return lax.dot_general(a, b, dims, preferred_element_type=f32)


def ends_of(len_ref):
    ends, total = [], jnp.int32(0)
    for j in range(len_ref.shape[1]):
        total = total + len_ref[0, j]
        ends.append(total)
    return ends


def segment_of(position, ends):
    member = jnp.zeros_like(position)
    for end in ends:
        member = member + (position >= end).astype(jnp.int32)
    return jnp.where(position < ends[-1], member, position + len(ends))


def key_range(ends, first, last, rows):
    low, high = jnp.int32(0), jnp.int32(0)
    start = jnp.int32(0)
    for end in ends:
        low = jnp.where((first >= start) & (first < end), start, low)
        high = jnp.where((last >= start) & (last < end), end, high)
        start = end
    total = ends[-1]
    low = jnp.where(first >= total, first, low)
    high = jnp.where(last >= total, last + 1, high)
    return low // KB, (high + KB - 1) // KB


def attend_forward_kernel(
    len_ref, x_ref, wq_ref, wk_ref, wv_ref, bq_ref, bv_ref,
    q_ref, k_ref, v_ref, mixed_ref, lse_ref,
    qs_ref, va_ref, acc_ref, top_ref,
):
    group = pl.program_id(0)
    rows, cols = q_ref.shape
    heads = cols // HD
    x = x_ref[...]
    query = (dot(x, wq_ref[...]) + bq_ref[...].astype(f32)).astype(bf16)
    q_ref[...] = query
    k_ref[...] = dot(x, wk_ref[...]).astype(bf16)
    value = (dot(x, wv_ref[...]) + bv_ref[...].astype(f32)).astype(bf16)
    v_ref[...] = value
    lane = lax.broadcasted_iota(jnp.int32, (rows, 128), 1)
    for h in range(heads):
        pair = slice(128 * (h // 2), 128 * (h // 2) + 128)
        own = (lane >= HD) if h % 2 else (lane < HD)
        qs_ref[h] = jnp.where(own, query[:, pair] * bf16(SCALE), bf16(0))
        va_ref[h] = jnp.where(own, value[:, pair], bf16(1))
    ends = ends_of(len_ref)

    @pl.when(group == 0)
    def _():
        lse_ref[...] = jnp.zeros_like(lse_ref)

    def q_step(qi, _):
        q_rows = pl.ds(pl.multiple_of(qi * QB, QB), QB)
        seg_q = segment_of(qi * QB + lax.broadcasted_iota(jnp.int32, (QB, 128), 0), ends)
        low, high = key_range(ends, qi * QB, qi * QB + QB - 1, rows)
        acc_ref[...] = jnp.zeros_like(acc_ref)
        top_ref[...] = jnp.full_like(top_ref, -3e38)

        def k_step(ki, _):
            k_rows = pl.ds(pl.multiple_of(ki * KB, KB), KB)
            seg_k = segment_of(ki * KB + lax.broadcasted_iota(jnp.int32, (1, KB), 1), ends)
            allowed = seg_q == seg_k
            for h in range(heads):
                pair = slice(128 * (h // 2), 128 * (h // 2) + 128)
                scores = dot(qs_ref[h, q_rows, :], k_ref[k_rows, pair], NT)
                scores = jnp.where(allowed, scores, MASKED)
                before = top_ref[h]
                top = jnp.maximum(before, jnp.max(scores, axis=1, keepdims=True))
                weights = jnp.exp(scores - top)
                acc_ref[h] = acc_ref[h] * jnp.exp(before - top) + dot(
                    weights.astype(bf16), va_ref[h, k_rows, :]
                )
                top_ref[h] = top
            return 0

        lax.fori_loop(low, high, k_step, 0)
        q_lane = lax.broadcasted_iota(jnp.int32, (QB, 128), 1)
        lse = lse_ref[q_rows, :]
        for p in range(heads // 2):
            out_a, out_b = acc_ref[2 * p], acc_ref[2 * p + 1]
            sum_a = pltpu.roll(out_a, HD, 1)
            sum_b = pltpu.roll(out_b, HD, 1)
            first = q_lane < HD
            mixed = jnp.where(first, out_a, out_b) / jnp.where(first, sum_a, sum_b)
            mixed_ref[q_rows, 128 * p : 128 * p + 128] = mixed.astype(bf16)
            head = group * heads + 2 * p
            lse = jnp.where(q_lane == head, top_ref[2 * p] + jnp.log(sum_a), lse)
            lse = jnp.where(q_lane == head + 1, top_ref[2 * p + 1] + jnp.log(out_b), lse)
        lse_ref[q_rows, :] = lse
        return 0

    lax.fori_loop(0, rows // QB, q_step, 0)


def attend_forward(lengths, tokens, full_qkv, bias_q, bias_v):
    rows, width = tokens.shape
    cols = 256
    groups = width // cols
    heads = cols // HD
    low = jax.ShapeDtypeStruct((rows, width), bf16)
    by_group = pl.BlockSpec((rows, cols), lambda g: (0, g))
    bias_spec = pl.BlockSpec((1, cols), lambda g: (0, g))
    return pl.pallas_call(
        attend_forward_kernel,
        grid=(groups,),
        in_specs=[
            pl.BlockSpec(memory_space=pltpu.SMEM),
            pl.BlockSpec((rows, width), lambda g: (0, 0)),
            pl.BlockSpec((width, cols), lambda g: (0, g)),
            pl.BlockSpec((width, cols), lambda g: (0, g + groups)),
            pl.BlockSpec((width, cols), lambda g: (0, g + 2 * groups)),
            bias_spec,
            bias_spec,
        ],
        out_specs=[by_group] * 4 + [pl.BlockSpec((rows, 128), lambda g: (0, 0))],
        out_shape=[low] * 4 + [jax.ShapeDtypeStruct((rows, 128), f32)],
        scratch_shapes=[
            pltpu.VMEM((heads, rows, 128), bf16),
            pltpu.VMEM((heads, rows, 128), bf16),
            pltpu.VMEM((heads, QB, 128), f32),
            pltpu.VMEM((heads, QB, 128), f32),
        ],
        compiler_params=pltpu.CompilerParams(vmem_limit_bytes=48 << 20),
        cost_estimate=pl.CostEstimate(flops=6 * rows * width * width, bytes_accessed=12 << 20, transcendentals=0),
        name="attend_forward",
    )(lengths, tokens, full_qkv, full_qkv, full_qkv, bias_q, bias_v)


def feed_forward_kernel(
    len_ref, x_ref, mixed_ref, cot_ref, wo_ref, wu_ref, wd_ref, vec_ref, bu_ref,
    out_ref, gp_ref, ga_ref, gm_ref, hl_ref, gb_ref, act_ref, gu_ref, gvec_ref, gbu_ref,
    slope_ref,
):
    step = pl.program_id(0)
    rows, width = x_ref.shape
    hidden_units = bu_ref.shape[1]

    @pl.when(step == 0)
    def _():
        gvec_ref[...] = jnp.zeros_like(gvec_ref)
        gbu_ref[...] = jnp.zeros_like(gbu_ref)

    total = ends_of(len_ref)[-1]
    position = step * rows + lax.broadcasted_iota(jnp.int32, (rows, 1), 0)
    valid = (position < total).astype(f32)

    def vec(i):
        return vec_ref[i : i + 1, :].astype(f32)

    def norm(values):
        centered = values - jnp.mean(values, axis=1, keepdims=True)
        scale = lax.rsqrt(jnp.mean(centered * centered, axis=1, keepdims=True) + NORM_EPS)
        return centered * scale, scale

    def norm_back(grad, gain, unit, scale):
        grad = grad * gain
        mean_grad = jnp.mean(grad, axis=1, keepdims=True)
        mean_unit = jnp.mean(grad * unit, axis=1, keepdims=True)
        return scale * (grad - mean_grad - unit * mean_unit)

    def add_vec(i, value):
        gvec_ref[i : i + 1, :] += jnp.sum(value, axis=0, keepdims=True)

    pre_one = x_ref[...].astype(f32) + dot(mixed_ref[...], wo_ref[...]) + vec(0)
    unit_one, scale_one = norm(pre_one)
    hidden = unit_one * vec(1) + vec(2)
    hidden_low = hidden.astype(bf16)
    hl_ref[...] = hidden_low
    branch = jnp.zeros((rows, width), f32)
    for f in range(hidden_units // FB):
        part = slice(f * FB, f * FB + FB)
        up = dot(hidden_low, wu_ref[:, part]) + bu_ref[:, part].astype(f32)
        bell = jnp.exp(up * up * -0.5)
        t = 1.0 / (1.0 + (0.3275911 * math.sqrt(0.5)) * jnp.abs(up))
        poly = 0.5 * 1.061405429 * t - 0.5 * 1.453152027
        poly = poly * t + 0.5 * 1.421413741
        poly = poly * t - 0.5 * 0.284496736
        poly = poly * t + 0.5 * 0.254829592
        tail = poly * t * bell
        share = jnp.where(up >= 0, 1.0 - tail, tail)
        active = (up * share).astype(bf16)
        act_ref[:, part] = active
        slope_ref[:, part] = share + up * bell * (1.0 / math.sqrt(2.0 * math.pi))
        branch = branch + dot(active, wd_ref[part, :])
    unit_two, scale_two = norm(hidden + branch + vec(3))
    out_ref[...] = (valid * (unit_two * vec(4) + vec(5))).astype(bf16)
    grad_out = valid * cot_ref[...].astype(f32)
    add_vec(0, grad_out * unit_two)
    add_vec(1, grad_out)
    grad_two = norm_back(grad_out, vec(4), unit_two, scale_two)
    grad_branch = grad_two.astype(bf16)
    gb_ref[...] = grad_branch
    add_vec(2, grad_branch.astype(f32))
    grad_hidden = grad_two
    for f in range(hidden_units // FB):
        part = slice(f * FB, f * FB + FB)
        grad_up = (dot(grad_branch, wd_ref[part, :], NT) * slope_ref[:, part]).astype(bf16)
        gu_ref[:, part] = grad_up
        gbu_ref[:, part] += jnp.sum(grad_up.astype(f32), axis=0, keepdims=True)
        grad_hidden = grad_hidden + dot(grad_up, wu_ref[:, part], NT)
    add_vec(3, grad_hidden * unit_one)
    add_vec(4, grad_hidden)
    grad_one = norm_back(grad_hidden, vec(1), unit_one, scale_one)
    gp_ref[...] = grad_one
    grad_attn = grad_one.astype(bf16)
    ga_ref[...] = grad_attn
    add_vec(5, grad_attn.astype(f32))
    gm_ref[...] = dot(grad_attn, wo_ref[...], NT).astype(bf16)


def feed_forward(lengths, tokens, mixed, cotangent, full_out, full_up, full_down, vecs, bias_up):
    rows, width = tokens.shape
    units = full_up.shape[1]
    by_rows = pl.BlockSpec((TB, width), lambda i: (i, 0))
    by_units = pl.BlockSpec((TB, units), lambda i: (i, 0))

    def whole(shape):
        return pl.BlockSpec(shape, lambda i: (0,) * len(shape), pipeline_mode=pl.Buffered(1))

    def kept(shape):
        return pl.BlockSpec(shape, lambda i: (0,) * len(shape))

    low = jax.ShapeDtypeStruct((rows, width), bf16)
    wide = jax.ShapeDtypeStruct((rows, units), bf16)
    return pl.pallas_call(
        feed_forward_kernel,
        grid=(rows // TB,),
        in_specs=[
            pl.BlockSpec(memory_space=pltpu.SMEM),
            by_rows, by_rows, by_rows,
            whole(full_out.shape), whole(full_up.shape), whole(full_down.shape),
            whole(vecs.shape), whole(bias_up.shape),
        ],
        out_specs=[by_rows] * 6 + [by_units] * 2 + [kept((8, width)), kept((1, units))],
        out_shape=[low, jax.ShapeDtypeStruct((rows, width), f32), low, low, low, low, wide, wide,
                   jax.ShapeDtypeStruct((8, width), f32), jax.ShapeDtypeStruct((1, units), f32)],
        scratch_shapes=[pltpu.VMEM((TB, units), f32)],
        compiler_params=pltpu.CompilerParams(vmem_limit_bytes=56 << 20),
        cost_estimate=pl.CostEstimate(flops=8 * rows * width * units + 4 * rows * width * width, bytes_accessed=40 << 20, transcendentals=0),
        name="feed_forward",
    )(lengths, tokens, mixed, cotangent, full_out, full_up, full_down, vecs, bias_up)


def weight_grad_kernel(place_ref, left_ref, right_ref, out_ref, left_t_ref, total_ref):
    @pl.when(pl.program_id(0) == 0)
    def _():
        left_t_ref[...] = left_ref[...].T

    total_ref[...] = dot(left_t_ref[...], right_ref[...])
    size = out_ref.shape[2]
    for b in range(out_ref.shape[0]):
        out_ref[place_ref[b], 0] = total_ref[b * size : b * size + size, :].astype(bf16)


def weight_grad_wide(place, left, right):
    rows, width = left.shape
    groups = right.shape[1] // width
    size = width // BLOCKS
    return pl.pallas_call(
        weight_grad_kernel,
        grid=(groups,),
        in_specs=[
            pl.BlockSpec(memory_space=pltpu.SMEM),
            pl.BlockSpec((rows, width), lambda g: (0, 0)),
            pl.BlockSpec((rows, width), lambda g: (0, g)),
        ],
        out_specs=pl.BlockSpec((BLOCKS, 1, size, width), lambda g: (0, g, 0, 0)),
        out_shape=jax.ShapeDtypeStruct((BLOCKS, groups, size, width), bf16),
        scratch_shapes=[pltpu.VMEM((width, rows), bf16), pltpu.VMEM((width, width), f32)],
        compiler_params=pltpu.CompilerParams(vmem_limit_bytes=40 << 20),
        cost_estimate=pl.CostEstimate(flops=2 * rows * width * right.shape[1], bytes_accessed=12 << 20, transcendentals=0),
        name="weight_grad_wide",
    )(place, left, right)


def weight_grad_tall_kernel(place_ref, left_ref, right_ref, out_ref, total_ref):
    total_ref[...] = dot(left_ref[...], right_ref[...], TN)
    size = out_ref.shape[1]
    base = pl.program_id(0) * (total_ref.shape[0] // size)
    for b in range(total_ref.shape[0] // size):
        out_ref[place_ref[base + b]] = total_ref[b * size : b * size + size, :].astype(bf16)


def weight_grad_tall(place, left, right):
    rows, units = left.shape
    width = right.shape[1]
    size = units // BLOCKS
    return pl.pallas_call(
        weight_grad_tall_kernel,
        grid=(units // width,),
        in_specs=[
            pl.BlockSpec(memory_space=pltpu.SMEM),
            pl.BlockSpec((rows, width), lambda g: (0, g)),
            pl.BlockSpec((rows, width), lambda g: (0, 0)),
        ],
        out_specs=pl.BlockSpec((BLOCKS, size, width), lambda g: (0, 0, 0)),
        out_shape=jax.ShapeDtypeStruct((BLOCKS, size, width), bf16),
        scratch_shapes=[pltpu.VMEM((width, width), f32)],
        compiler_params=pltpu.CompilerParams(vmem_limit_bytes=40 << 20),
        cost_estimate=pl.CostEstimate(flops=2 * rows * width * units, bytes_accessed=12 << 20, transcendentals=0),
        name="weight_grad_tall",
    )(place, left, right)


def attend_backward_kernel(
    len_ref, place_ref, x_ref, q_ref, k_ref, v_ref, do_ref, o_ref, lse_ref,
    dq_ref, dk_ref, dv_ref, gw_ref, gbias_ref,
    xt_ref, qs_ref, dos_ref, kt_ref, lse_t_ref, delta_ref, dqt_ref, dk_acc, dv_acc, total_ref,
):
    group = pl.program_id(0)
    rows, cols = q_ref.shape
    heads = cols // HD

    @pl.when(group == 0)
    def _():
        xt_ref[...] = x_ref[...].T
        lse_t_ref[...] = lse_ref[...].T

    query, keys, values, grad = q_ref[...], k_ref[...], v_ref[...], do_ref[...]
    lane = lax.broadcasted_iota(jnp.int32, (rows, 128), 1)
    for h in range(heads):
        pair = slice(128 * (h // 2), 128 * (h // 2) + 128)
        own = (lane >= HD) if h % 2 else (lane < HD)
        qs_ref[h] = jnp.where(own, query[:, pair] * bf16(SCALE), bf16(0))
        dos_ref[h] = jnp.where(own, grad[:, pair], bf16(0))
    kt_ref[...] = keys.T
    product = grad.astype(f32) * o_ref[...].astype(f32)
    high_part = product.astype(bf16)
    low_part = (product - high_part.astype(f32)).astype(bf16)
    pick = (
        lax.broadcasted_iota(jnp.int32, (8, cols), 1) // HD
        == lax.broadcasted_iota(jnp.int32, (8, cols), 0)
    ).astype(bf16)
    delta_ref[...] = dot(pick, high_part, NT) + dot(pick, low_part, NT)
    dk_acc[...] = jnp.zeros_like(dk_acc)
    dv_acc[...] = jnp.zeros_like(dv_acc)
    ends = ends_of(len_ref)

    def q_step(qi, _):
        q_start = pl.multiple_of(qi * QB, QB)
        q_rows = pl.ds(q_start, QB)
        seg_q = segment_of(qi * QB + lax.broadcasted_iota(jnp.int32, (1, QB), 1), ends)
        low, high = key_range(ends, qi * QB, qi * QB + QB - 1, rows)
        dqt_ref[...] = jnp.zeros_like(dqt_ref)

        def k_step(ki, _):
            k_rows = pl.ds(pl.multiple_of(ki * KB, KB), KB)
            seg_k = segment_of(ki * KB + lax.broadcasted_iota(jnp.int32, (KB, 128), 0), ends)
            allowed = jnp.concatenate([seg_k] * (QB // 128), axis=1) == seg_q
            for p in range(heads // 2):
                pair = slice(128 * p, 128 * p + 128)
                probs_pair, grads_pair = [], []
                for h in (2 * p, 2 * p + 1):
                    scores = dot(k_ref[k_rows, pair], qs_ref[h, q_rows, :], NT)
                    log_total = lse_t_ref[pl.ds(group * heads + h, 1), q_rows]
                    probs = jnp.exp(jnp.where(allowed, scores, MASKED) - log_total)
                    grad_probs = dot(v_ref[k_rows, pair], dos_ref[h, q_rows, :], NT)
                    grad_scores = (probs * (grad_probs - delta_ref[h : h + 1, q_rows])).astype(bf16)
                    probs_pair.append(probs.astype(bf16))
                    grads_pair.append(grad_scores)
                    dqt_ref[h * HD : h * HD + HD, :] += dot(
                        kt_ref[h * HD : h * HD + HD, k_rows], grad_scores
                    )
                dv_acc[k_rows, pair] += dot(probs_pair[0], dos_ref[2 * p, q_rows, :]) + dot(
                    probs_pair[1], dos_ref[2 * p + 1, q_rows, :]
                )
                dk_acc[k_rows, pair] += dot(grads_pair[0], qs_ref[2 * p, q_rows, :]) + dot(
                    grads_pair[1], qs_ref[2 * p + 1, q_rows, :]
                )
            return 0

        lax.fori_loop(low, high, k_step, 0)
        dq_ref[q_rows, :] = (dqt_ref[...] * SCALE).T.astype(bf16)
        return 0

    lax.fori_loop(0, rows // QB, q_step, 0)
    dk_ref[...] = dk_acc[...].astype(bf16)
    dv_ref[...] = dv_acc[...].astype(bf16)
    size = gw_ref.shape[2]
    for s, part in enumerate((dq_ref, dk_ref, dv_ref)):
        total_ref[...] = dot(xt_ref[...], part[...])
        for b in range(BLOCKS):
            gw_ref[place_ref[b], s] = total_ref[b * size : b * size + size, :].astype(bf16)
    gbias_ref[0:1, :] = jnp.sum(dq_ref[...].astype(f32), axis=0, keepdims=True)
    gbias_ref[1:2, :] = jnp.sum(dv_ref[...].astype(f32), axis=0, keepdims=True)


def attend_backward(lengths, place, tokens, query, keys, values, grad_mixed, mixed, lse):
    rows, width = tokens.shape
    cols = 256
    groups = width // cols
    heads = cols // HD
    size = width // BLOCKS
    by_group = pl.BlockSpec((rows, cols), lambda g: (0, g))
    low = jax.ShapeDtypeStruct((rows, width), bf16)
    return pl.pallas_call(
        attend_backward_kernel,
        grid=(groups,),
        in_specs=[
            pl.BlockSpec(memory_space=pltpu.SMEM),
            pl.BlockSpec(memory_space=pltpu.SMEM),
            pl.BlockSpec((rows, width), lambda g: (0, 0)),
        ]
        + [by_group] * 5
        + [pl.BlockSpec((rows, 128), lambda g: (0, 0))],
        out_specs=[by_group] * 3
        + [
            pl.BlockSpec((BLOCKS, 3, size, cols), lambda g: (0, 0, 0, g)),
            pl.BlockSpec((8, cols), lambda g: (0, g)),
        ],
        out_shape=[low] * 3
        + [
            jax.ShapeDtypeStruct((BLOCKS, 3, size, width), bf16),
            jax.ShapeDtypeStruct((8, width), f32),
        ],
        scratch_shapes=[
            pltpu.VMEM((width, rows), bf16),
            pltpu.VMEM((heads, rows, 128), bf16),
            pltpu.VMEM((heads, rows, 128), bf16),
            pltpu.VMEM((cols, rows), bf16),
            pltpu.VMEM((128, rows), f32),
            pltpu.VMEM((8, rows), f32),
            pltpu.VMEM((cols, QB), f32),
            pltpu.VMEM((rows, cols), f32),
            pltpu.VMEM((rows, cols), f32),
            pltpu.VMEM((width, cols), f32),
        ],
        compiler_params=pltpu.CompilerParams(vmem_limit_bytes=48 << 20),
        cost_estimate=pl.CostEstimate(flops=20 * rows * width * width, bytes_accessed=16 << 20, transcendentals=0),
        name="attend_backward",
    )(lengths, place, tokens, query, keys, values, grad_mixed, mixed, lse)


def token_grad_kernel(gp_ref, dq_ref, dk_ref, dv_ref, w_ref, out_ref):
    width = gp_ref.shape[1]
    out_ref[...] = (
        gp_ref[...]
        + dot(dq_ref[...], w_ref[:, :width], NT)
        + dot(dk_ref[...], w_ref[:, width : 2 * width], NT)
        + dot(dv_ref[...], w_ref[:, 2 * width :], NT)
    )


def token_grad(grad_one, dq, dk, dv, full_qkv):
    rows, width = grad_one.shape
    by_rows = pl.BlockSpec((TB, width), lambda i: (i, 0))
    return pl.pallas_call(
        token_grad_kernel,
        grid=(rows // TB,),
        in_specs=[by_rows] * 4
        + [pl.BlockSpec(full_qkv.shape, lambda i: (0, 0), pipeline_mode=pl.Buffered(1))],
        out_specs=by_rows,
        out_shape=jax.ShapeDtypeStruct((rows, width), f32),
        compiler_params=pltpu.CompilerParams(vmem_limit_bytes=40 << 20),
        cost_estimate=pl.CostEstimate(flops=6 * rows * width * width, bytes_accessed=14 << 20, transcendentals=0),
        name="token_grad",
    )(grad_one, dq, dk, dv, full_qkv)


CORE, X, Y, Z_LOW, Z_HIGH = 1, 2, 4, 8, 16


def relative_places():
    places = np.zeros((32, 32), np.int32)
    for i in range(32):
        for b in range(32):
            bits = i ^ b
            x, y = int(bits & X > 0), int(bits & Y > 0)
            first, second = (y, x) if b & CORE else (x, y)
            low, high = int(bits & Z_LOW > 0), int(bits & Z_HIGH > 0)
            places[i, b] = 16 * (bits & CORE) + 8 * first + 4 * second + 2 * low + high
    return places


def exchange(values, even, odd):
    return lax.ppermute(
        values, "dp", [(i, i ^ (odd if i & CORE else even)) for i in range(32)]
    )


def added(a, b):
    return (a.astype(f32) + b.astype(f32)).astype(bf16)


def reduce_blocks(parts):
    halves = [part.reshape(2, 16, *part.shape[1:]) for part in parts]
    received = [exchange(half[1], CORE, CORE) for half in halves]

    def joined(rows):
        return jnp.concatenate(
            [added(half[0, rows], got[rows]) for half, got in zip(halves, received)], axis=1
        )

    send, keep = joined(slice(8, 16)), joined(slice(0, 8))
    for even, odd in ((X, Y), (Y, X), (Z_LOW, Z_LOW)):
        got = exchange(send, even, odd)
        half = keep.shape[0] // 2
        send, keep = added(keep[half:], got[half:]), added(keep[:half], got[:half])
    got = exchange(send, Z_HIGH, Z_HIGH)
    return keep[0].astype(f32) + got[0].astype(f32)


def body(
    tokens, cotangent, lengths, w_qkv, w_out, w_up, w_down, bias_q, bias_v, bias_out,
    gain_one, shift_one, bias_up, bias_down, gain_two, shift_two,
):
    count = lax.axis_size("dp")
    index = lax.axis_index("dp")
    width = tokens.shape[1]
    units = w_up.shape[1]
    shard = w_qkv.shape[0]
    ratio = units // width
    small = jnp.stack(
        [bias_q, bias_v, bias_out, gain_one, shift_one, bias_down, gain_two, shift_two], axis=1
    )
    small = jnp.concatenate([small, bias_up.reshape(shard, ratio)], axis=1)
    small = jnp.pad(small, ((0, 0), (0, 128 - small.shape[1])))
    attn = lax.all_gather(jnp.concatenate([w_qkv, small], axis=1), "dp", axis=0, tiled=True)
    rest = lax.all_gather(
        jnp.concatenate([w_out, w_up, w_down.reshape(shard, ratio * width)], axis=1),
        "dp", axis=0, tiled=True,
    )
    full_qkv = attn[:, : 3 * width]
    vectors = attn[:, 3 * width :]
    rows8 = vectors[:, :8].T
    full_bias_up = vectors[:, 8 : 8 + ratio].reshape(1, units)
    full_out = rest[:, :width]
    full_up = rest[:, width : width + units]
    full_down = rest[:, width + units :].reshape(units, width)
    vecs = jnp.concatenate([rows8[2:], rows8[:2]], axis=0)

    query, keys, values, mixed, lse = attend_forward(
        lengths, tokens, full_qkv, rows8[0:1], rows8[1:2]
    )
    output, grad_one, grad_attn, grad_mixed, hidden_low, grad_branch, active, grad_up, gvec, gbu = (
        feed_forward(lengths, tokens, mixed, cotangent, full_out, full_up, full_down, vecs, full_bias_up)
    )
    if count == BLOCKS:
        table = relative_places()
        place = jnp.asarray(table)[index]
        blocks_at = jnp.asarray(np.argsort(table, axis=1))[index]
    else:
        place = jnp.arange(BLOCKS, dtype=jnp.int32)
    part_down = weight_grad_tall(place, active, grad_branch)
    part_up = weight_grad_wide(place, hidden_low, grad_up)
    part_out = weight_grad_wide(place, mixed, grad_attn)
    dq, dk, dv, part_qkv, gbias = attend_backward(
        lengths, place, tokens, query, keys, values, grad_mixed, mixed, lse
    )
    grad_tokens = token_grad(grad_one, dq, dk, dv, full_qkv)
    if count != BLOCKS:
        def scattered(part):
            return lax.psum_scatter(part, "dp", scatter_dimension=0, tiled=True).astype(f32)

        def lined(part):
            return part.transpose(0, 2, 1, 3).reshape(width, -1)

        lines = jnp.concatenate([gvec, gbias[:2], gbu.reshape(ratio, width)], axis=0)
        return (
            output, grad_tokens, scattered(lined(part_qkv)), scattered(lined(part_out)),
            scattered(lined(part_up)), scattered(part_down.reshape(units, width)),
            scattered(gbias[0]), scattered(gbias[1]), scattered(gvec[5]), scattered(gvec[3]),
            scattered(gvec[4]), scattered(gbu[0]), scattered(gvec[2]), scattered(gvec[0]),
            scattered(gvec[1]),
        )

    def small_part(lines):
        line = jnp.concatenate([row.reshape(BLOCKS, -1) for row in lines], axis=1)
        line = jnp.pad(line.astype(bf16), ((0, 0), (0, width - line.shape[1])))
        return jnp.pad(line[blocks_at][:, None, :], ((0, 0), (0, 7), (0, 0)))

    def rows_of(part):
        return part.reshape(BLOCKS, -1, width)

    small_mlp = small_part([*gvec[:6], gbu[0]])
    mlp = reduce_blocks([part_down, rows_of(part_up), small_mlp])
    small_attn = small_part([*gbias[:2]])
    rest = reduce_blocks([rows_of(part_qkv), rows_of(part_out), small_attn])

    def wide_of(rows):
        return rows.reshape(-1, shard, width).transpose(1, 0, 2).reshape(shard, -1)

    tall = ratio * shard
    line = mlp[2 * tall]
    line_attn = rest[4 * shard]

    def piece(line, i):
        return line[i * shard : i * shard + shard]

    return (
        output, grad_tokens, wide_of(rest[: 3 * shard]), rest[3 * shard : 4 * shard],
        wide_of(mlp[tall : 2 * tall]), mlp[:tall],
        piece(line_attn, 0), piece(line_attn, 1), piece(line, 5), piece(line, 3), piece(line, 4),
        line[6 * shard : 6 * shard + tall], piece(line, 2), piece(line, 0), piece(line, 1),
    )


def solution(mesh):
    rows, vector = P("dp", None), P("dp")
    return jax.shard_map(
        body, mesh=mesh, in_specs=(rows,) * 7 + (vector,) * 9, out_specs=(rows,) * 6 + (vector,) * 9,
        check_vma=False,
    )
```

```python
import functools
import math

import jax
import jax.numpy as jnp
import numpy as np
from jax import lax
from jax.experimental import pallas as pl
from jax.experimental.pallas import tpu as pltpu
from jax.sharding import PartitionSpec as P

HD = 64
FORWARD_TILE = 512
BACKWARD_TILE = 256
FAR = 2.0**30
BITS = 11
COLS = 256
TB = 256
FB = 768
BLOCKS = 32
NORM_EPS = 1e-06
SCALE = 1.0 / math.sqrt(HD)
NT = (((1,), (1,)), ((), ()))
TN = (((0,), (0,)), ((), ()))
f32 = jnp.float32
bf16 = jnp.bfloat16


def dot(a, b, dims=(((1,), (0,)), ((), ()))):
    return lax.dot_general(a, b, dims, preferred_element_type=f32)


def ends_of(len_ref):
    ends, total = [], jnp.int32(0)
    for j in range(len_ref.shape[1]):
        total = total + len_ref[0, j]
        ends.append(total)
    return ends


def segment_of(position, ends):
    member = jnp.zeros_like(position)
    for end in ends:
        member = member + (position >= end).astype(jnp.int32)
    return jnp.where(position < ends[-1], member, position + len(ends))


def key_range(ends, first, last, tile):
    low, high = jnp.int32(0), jnp.int32(0)
    start = jnp.int32(0)
    for end in ends:
        low = jnp.where((first >= start) & (first < end), start, low)
        high = jnp.where((last >= start) & (last < end), end, high)
        start = end
    total = ends[-1]
    low = jnp.where(first >= total, first, low)
    high = jnp.where(last >= total, last + 1, high)
    return low // tile, (high + tile - 1) // tile


def other_half(own, other, h):
    return jnp.concatenate([other, own] if h % 2 else [own, other], axis=0)


def segment_codes(rows, ends):
    spot = lax.broadcasted_iota(jnp.int32, (HD, rows), 0)
    seg = segment_of(lax.broadcasted_iota(jnp.int32, (1, rows), 1), ends)
    bit = (seg >> (spot // 2)) & 1
    code_q = jnp.where(spot < 2 * BITS, jnp.where(spot % 2 == 0, bit, 1 - bit), 0)
    spot = lax.broadcasted_iota(jnp.int32, (rows, 128), 1) % HD
    seg = segment_of(lax.broadcasted_iota(jnp.int32, (rows, 128), 0), ends)
    bit = (seg >> (spot // 2)) & 1
    code_k = jnp.where(spot < 2 * BITS, jnp.where(spot % 2 == 0, 1 - bit, bit), 0)
    return code_q.astype(f32).astype(bf16), code_k.astype(f32) * -FAR


def pieces(value):
    high = value.astype(bf16)
    rest = value - high.astype(f32)
    middle = rest.astype(bf16)
    return [high, middle, (rest - middle.astype(f32)).astype(bf16)]


def attend_forward_kernel(
    group, len_ref, x_ref, wq_ref, wk_ref, wv_ref, vec_ref,
    q_ref, k_ref, v_ref, mixed_ref, lse_ref,
    qt_ref, ka_ref, vt_ref, code_q_ref, code_k_ref, acc_ref, top_ref, bias_ref,
):
    ends = ends_of(len_ref)

    code_q_ref[...], code_k = segment_codes(q_ref.shape[0], ends)
    code_k_ref[...] = code_k.astype(bf16)
    bias_ref[...] = vec_ref[...].astype(f32).T[:8]

    rows, cols = q_ref.shape
    heads = cols // HD
    own_cols = slice(group * cols, group * cols + cols)
    x = x_ref[...]
    query = (dot(x, wq_ref[...]) + bias_ref[0:1, own_cols]).astype(bf16)
    q_ref[...] = query
    keys = dot(x, wk_ref[...]).astype(bf16)
    k_ref[...] = keys
    value = (dot(x, wv_ref[...]) + bias_ref[1:2, own_cols]).astype(bf16)
    v_ref[...] = value
    turned, turned_value = (query * bf16(SCALE)).T, value.T
    lane = lax.broadcasted_iota(jnp.int32, (rows, 128), 1)
    for h in range(heads):
        part = slice(h * HD, h * HD + HD)
        own = (lane >= HD) if h % 2 else (lane < HD)
        qt_ref[h] = other_half(turned[part], code_q_ref[...], h)
        ka_ref[h] = jnp.where(own, keys[:, 128 * (h // 2) : 128 * (h // 2) + 128], code_k_ref[...])
        vt_ref[h, :HD] = turned_value[part]
        vt_ref[h, HD:] = jnp.ones((16, rows), bf16)

    def q_step(qi, _):
        q_cols = pl.ds(pl.multiple_of(qi * FORWARD_TILE, FORWARD_TILE), FORWARD_TILE)
        low, high = key_range(ends, qi * FORWARD_TILE, qi * FORWARD_TILE + FORWARD_TILE - 1, FORWARD_TILE)
        acc_ref[...] = jnp.zeros_like(acc_ref)
        top_ref[...] = jnp.full_like(top_ref, -3e38)

        def k_step(ki, _):
            k_rows = pl.ds(pl.multiple_of(ki * FORWARD_TILE, FORWARD_TILE), FORWARD_TILE)
            tops = top_ref[...]
            new_tops = []

            def scores_of(h):
                return dot(ka_ref[h, k_rows, :], qt_ref[h, :, q_cols])

            ahead = [scores_of(h) for h in range(1)]
            pending = []

            def finish(h, low_weights, fade):
                acc_ref[h] = acc_ref[h] * fade + dot(vt_ref[h, :, k_rows], low_weights)

            for h in range(heads):
                if h + 1 < heads:
                    ahead.append(scores_of(h + 1))
                scores = ahead[h]
                ahead[h] = None
                before = tops[h : h + 1]
                top = jnp.maximum(before, jnp.max(scores, axis=0, keepdims=True))
                new_tops.append(top)
                pending.append((h, jnp.exp(scores - top).astype(bf16), jnp.exp(before - top)))
                if len(pending) > 0:
                    finish(*pending.pop(0))
            for item in pending:
                finish(*item)
            spare = [jnp.zeros((8 - heads, FORWARD_TILE), f32)]
            top_ref[...] = jnp.concatenate(new_tops + spare, axis=0)
            return 0

        lax.fori_loop(low, high, k_step, 0)
        totals = jnp.concatenate([acc_ref[h, HD : HD + 1] for h in range(heads)], axis=0)
        for p in range(heads // 2):
            halves = [acc_ref[h, :HD] / totals[h : h + 1] for h in (2 * p, 2 * p + 1)]
            mixed = jnp.concatenate(halves, axis=0)
            mixed_ref[q_cols, 128 * p : 128 * p + 128] = mixed.T.astype(bf16)
        lse = top_ref[0:heads] + jnp.log(totals)
        lse_ref[0, :, q_cols] = jnp.concatenate([lse, jnp.zeros((8 - heads, FORWARD_TILE), f32)], axis=0)
        return 0

    lax.fori_loop(0, rows // FORWARD_TILE, q_step, 0)


def attend_forward(group, lengths, tokens, full_qkv):
    rows, width = tokens.shape
    cols = COLS
    groups = width // cols
    heads = cols // HD
    low = jax.ShapeDtypeStruct((rows, cols), bf16)
    own = pl.BlockSpec((rows, cols), lambda g: (0, 0))
    return pl.pallas_call(
        functools.partial(attend_forward_kernel, group),
        grid=(1,),
        in_specs=[
            pl.BlockSpec(memory_space=pltpu.SMEM),
            pl.BlockSpec((rows, width), lambda g: (0, 0)),
            pl.BlockSpec((width, cols), lambda g: (0, group)),
            pl.BlockSpec((width, cols), lambda g: (0, group + groups)),
            pl.BlockSpec((width, cols), lambda g: (0, group + 2 * groups)),
            pl.BlockSpec((width, 128), lambda g: (0, 3 * width // 128)),
        ],
        out_specs=[own] * 4 + [pl.BlockSpec((1, 8, rows), lambda g: (0, 0, 0))],
        out_shape=[low] * 4 + [jax.ShapeDtypeStruct((1, 8, rows), f32)],
        scratch_shapes=[
            pltpu.VMEM((heads, 128, rows), bf16),
            pltpu.VMEM((heads, rows, 128), bf16),
            pltpu.VMEM((heads, HD + 16, rows), bf16),
            pltpu.VMEM((HD, rows), bf16),
            pltpu.VMEM((rows, 128), bf16),
            pltpu.VMEM((heads, HD + 16, FORWARD_TILE), f32),
            pltpu.VMEM((8, FORWARD_TILE), f32),
            pltpu.VMEM((8, width), f32),
        ],
        compiler_params=pltpu.CompilerParams(vmem_limit_bytes=44 << 20),
        cost_estimate=pl.CostEstimate(flops=12 * rows * width * width, bytes_accessed=12 << 20, transcendentals=0),
        name="attend_forward",
    )(lengths, tokens, full_qkv, full_qkv, full_qkv, full_qkv)


def feed_forward_kernel(
    len_ref, x_ref, mixed_a_ref, mixed_b_ref, mixed_c_ref, cot_ref, wo_ref, wu_ref, wd_ref, vec_ref, bu_ref,
    out_ref, gp_ref, ga_ref, gm_ref, hl_ref, gb_ref, mixed_ref, act_ref, gu_ref, gvec_ref, gbu_ref,
    slope_ref, rows_ref,
):
    step = pl.program_id(0)
    rows, width = x_ref.shape
    hidden_units = bu_ref.shape[1]

    @pl.when(step == 0)
    def _():
        gvec_ref[...] = jnp.zeros_like(gvec_ref)
        gbu_ref[...] = jnp.zeros_like(gbu_ref)
        rows_ref[...] = vec_ref[...].astype(f32).T[:8]

    total = ends_of(len_ref)[-1]
    position = step * rows + lax.broadcasted_iota(jnp.int32, (rows, 1), 0)
    valid = (position < total).astype(f32)

    def vec(i):
        return rows_ref[i + 2 : i + 3, :]

    def norm(values):
        centered = values - jnp.mean(values, axis=1, keepdims=True)
        scale = lax.rsqrt(jnp.mean(centered * centered, axis=1, keepdims=True) + NORM_EPS)
        return centered * scale, scale

    def norm_back(grad, gain, unit, scale):
        grad = grad * gain
        mean_grad = jnp.mean(grad, axis=1, keepdims=True)
        mean_unit = jnp.mean(grad * unit, axis=1, keepdims=True)
        return scale * (grad - mean_grad - unit * mean_unit)

    def add_vec(i, value):
        gvec_ref[i : i + 1, :] += jnp.sum(value, axis=0, keepdims=True)

    mixed_ref[...] = jnp.concatenate(
        [mixed_a_ref[...], mixed_b_ref[...], mixed_c_ref[...]], axis=1
    )
    pre_one = x_ref[...].astype(f32) + dot(mixed_ref[...], wo_ref[...]) + vec(0)
    unit_one, scale_one = norm(pre_one)
    hidden = unit_one * vec(1) + vec(2)
    hidden_low = hidden.astype(bf16)
    hl_ref[...] = hidden_low
    branch = jnp.zeros((rows, width), f32)
    for f in range(hidden_units // FB):
        part = slice(f * FB, f * FB + FB)
        up = dot(hidden_low, wu_ref[:, part]) + bu_ref[:, part].astype(f32)
        bell = jnp.exp(up * up * -0.5)
        t = 1.0 / (1.0 + (0.3275911 * math.sqrt(0.5)) * jnp.abs(up))
        poly = 0.5 * 1.061405429 * t - 0.5 * 1.453152027
        poly = poly * t + 0.5 * 1.421413741
        poly = poly * t - 0.5 * 0.284496736
        poly = poly * t + 0.5 * 0.254829592
        tail = poly * t * bell
        share = jnp.where(up >= 0, 1.0 - tail, tail)
        active = (up * share).astype(bf16)
        act_ref[:, part] = active
        slope_ref[:, part] = share + up * bell * (1.0 / math.sqrt(2.0 * math.pi))
        branch = branch + dot(active, wd_ref[part, :])
    unit_two, scale_two = norm(hidden + branch + vec(3))
    out_ref[...] = (valid * (unit_two * vec(4) + vec(5))).astype(bf16)
    grad_out = valid * cot_ref[...].astype(f32)
    add_vec(0, grad_out * unit_two)
    add_vec(1, grad_out)
    grad_two = norm_back(grad_out, vec(4), unit_two, scale_two)
    grad_branch = grad_two.astype(bf16)
    gb_ref[...] = grad_branch
    add_vec(2, grad_branch.astype(f32))
    grad_hidden = grad_two
    for f in range(hidden_units // FB):
        part = slice(f * FB, f * FB + FB)
        grad_up = (dot(grad_branch, wd_ref[part, :], NT) * slope_ref[:, part]).astype(bf16)
        gu_ref[:, part] = grad_up
        gbu_ref[:, part] += jnp.sum(grad_up.astype(f32), axis=0, keepdims=True)
        grad_hidden = grad_hidden + dot(grad_up, wu_ref[:, part], NT)
    add_vec(3, grad_hidden * unit_one)
    add_vec(4, grad_hidden)
    grad_one = norm_back(grad_hidden, vec(1), unit_one, scale_one)
    gp_ref[...] = grad_one
    grad_attn = grad_one.astype(bf16)
    ga_ref[...] = grad_attn
    add_vec(5, grad_attn.astype(f32))
    gm_ref[...] = dot(grad_attn, wo_ref[...], NT).astype(bf16)


def feed_forward(lengths, tokens, mixed, cotangent, full_up_out, full_down, full_qkv, bias_up):
    rows, width = tokens.shape
    units = bias_up.shape[1]
    by_rows = pl.BlockSpec((TB, width), lambda i: (i, 0))
    by_units = pl.BlockSpec((TB, units), lambda i: (i, 0))

    def whole(shape, column=0):
        return pl.BlockSpec(shape, lambda i: (0, column), pipeline_mode=pl.Buffered(1))

    def kept(shape):
        return pl.BlockSpec(shape, lambda i: (0,) * len(shape))

    low = jax.ShapeDtypeStruct((rows, width), bf16)
    wide = jax.ShapeDtypeStruct((rows, units), bf16)
    return pl.pallas_call(
        feed_forward_kernel,
        grid=(rows // TB,),
        in_specs=[
            pl.BlockSpec(memory_space=pltpu.SMEM),
            by_rows, *[pl.BlockSpec((TB, part.shape[1]), lambda i: (i, 0)) for part in mixed], by_rows,
            whole((width, width), units // width), whole((width, units)), whole(full_down.shape),
            whole((width, 128), 3 * width // 128), whole(bias_up.shape),
        ],
        out_specs=[by_rows] * 7 + [by_units] * 2 + [kept((8, width)), kept((1, units))],
        out_shape=[low, jax.ShapeDtypeStruct((rows, width), f32), low, low, low, low, low, wide, wide,
                   jax.ShapeDtypeStruct((8, width), f32), jax.ShapeDtypeStruct((1, units), f32)],
        scratch_shapes=[pltpu.VMEM((TB, units), f32), pltpu.VMEM((8, width), f32)],
        compiler_params=pltpu.CompilerParams(vmem_limit_bytes=56 << 20),
        cost_estimate=pl.CostEstimate(flops=8 * rows * width * units + 4 * rows * width * width, bytes_accessed=40 << 20, transcendentals=0),
        name="feed_forward",
    )(lengths, tokens, *mixed, cotangent, full_up_out, full_up_out, full_down, full_qkv, bias_up)


def store_blocks(place_ref, total_ref, near_ref, far_ref, at, base=0):
    size = near_ref.shape[-2]
    own = place_ref[BLOCKS]
    for pair in range(total_ref.shape[0] // (2 * size)):
        for ref, core in ((near_ref, own), (far_ref, 1 - own)):
            block = 2 * pair + core
            rows = pl.ds(pl.multiple_of(block * size, size), size)
            ref[(place_ref[base + block] % (BLOCKS // 2), *at)] = total_ref[rows, :].astype(bf16)


def weight_grad_kernel(place_ref, left_ref, right_ref, near_ref, far_ref, left_t_ref, total_ref):
    @pl.when(pl.program_id(0) == 0)
    def _():
        left_t_ref[...] = left_ref[...].T

    total_ref[...] = dot(left_t_ref[...], right_ref[...])
    store_blocks(place_ref, total_ref, near_ref, far_ref, (0,))


def weight_grad_wide(place, left, right, cols):
    rows, width = left.shape
    groups = right.shape[1] // cols
    size = width // BLOCKS
    return pl.pallas_call(
        weight_grad_kernel,
        grid=(groups,),
        in_specs=[
            pl.BlockSpec(memory_space=pltpu.SMEM),
            pl.BlockSpec((rows, width), lambda g: (0, 0)),
            pl.BlockSpec((rows, cols), lambda g: (0, g)),
        ],
        out_specs=[pl.BlockSpec((BLOCKS // 2, 1, size, cols), lambda g: (0, g, 0, 0))] * 2,
        out_shape=[jax.ShapeDtypeStruct((BLOCKS // 2, groups, size, cols), bf16)] * 2,
        scratch_shapes=[pltpu.VMEM((width, rows), bf16), pltpu.VMEM((width, cols), f32)],
        compiler_params=pltpu.CompilerParams(vmem_limit_bytes=20 << 20),
        cost_estimate=pl.CostEstimate(flops=2 * rows * width * right.shape[1], bytes_accessed=12 << 20, transcendentals=0),
        name="weight_grad_wide",
    )(place, left, right)


def weight_grad_tall_kernel(place_ref, left_ref, right_ref, near_ref, far_ref, total_ref):
    total_ref[...] = dot(left_ref[...], right_ref[...], TN)
    base = pl.program_id(0) * (total_ref.shape[0] // near_ref.shape[1])
    store_blocks(place_ref, total_ref, near_ref, far_ref, (), base)


def weight_grad_tall(place, left, right):
    rows, units = left.shape
    width = right.shape[1]
    size = units // BLOCKS
    return pl.pallas_call(
        weight_grad_tall_kernel,
        grid=(units // width,),
        in_specs=[
            pl.BlockSpec(memory_space=pltpu.SMEM),
            pl.BlockSpec((rows, width), lambda g: (0, g)),
            pl.BlockSpec((rows, width), lambda g: (0, 0)),
        ],
        out_specs=[pl.BlockSpec((BLOCKS // 2, size, width), lambda g: (0, 0, 0))] * 2,
        out_shape=[jax.ShapeDtypeStruct((BLOCKS // 2, size, width), bf16)] * 2,
        scratch_shapes=[pltpu.VMEM((width, width), f32)],
        compiler_params=pltpu.CompilerParams(vmem_limit_bytes=20 << 20),
        cost_estimate=pl.CostEstimate(flops=2 * rows * width * units, bytes_accessed=12 << 20, transcendentals=0),
        name="weight_grad_tall",
    )(place, left, right)


def attend_backward_kernel(
    len_ref, place_ref, x_ref, q_ref, k_ref, v_ref, do_ref, o_ref, lse_ref,
    dq_ref, dk_ref, dv_ref, near_ref, far_ref, gbias_ref,
    xt_ref, qs_ref, dos_ref, qt_ref, dot_ref, ka_ref, va_ref, kt_ref, code_q_ref, code_k_ref,
    dqt_ref, dk_acc, dv_acc, total_ref,
):
    rows, cols = q_ref.shape
    heads = cols // HD
    ends = ends_of(len_ref)

    xt_ref[...] = x_ref[...].T
    code_q, code_k = segment_codes(rows, ends)
    code_q_ref[...] = code_q
    spot = lax.broadcasted_iota(jnp.int32, (rows, 128), 1) % HD
    code_k_ref[...] = jnp.where((spot >= 2 * BITS) & (spot < 2 * BITS + 3), 1.0, code_k).astype(bf16)

    query, keys, values, grad = q_ref[...], k_ref[...], v_ref[...], do_ref[...]
    lane = lax.broadcasted_iota(jnp.int32, (rows, 128), 1)
    for h in range(heads):
        pair = slice(128 * (h // 2), 128 * (h // 2) + 128)
        own = (lane >= HD) if h % 2 else (lane < HD)
        qs_ref[h] = jnp.where(own, query[:, pair] * bf16(SCALE), bf16(0))
        dos_ref[h] = jnp.where(own, grad[:, pair], bf16(0))
    kt_ref[...] = keys.T
    product = grad.astype(f32) * o_ref[...].astype(f32)
    high_part = product.astype(bf16)
    low_part = (product - high_part.astype(f32)).astype(bf16)
    pick = (
        lax.broadcasted_iota(jnp.int32, (8, cols), 1) // HD
        == lax.broadcasted_iota(jnp.int32, (8, cols), 0)
    ).astype(bf16)
    delta = dot(pick, high_part, NT) + dot(pick, low_part, NT)
    turned, turned_grad = (query * bf16(SCALE)).T, grad.T
    lane = lax.broadcasted_iota(jnp.int32, (rows, 128), 1)
    ones = jnp.where(lane % HD < 3, 1.0, 0.0).astype(bf16)
    for h in range(heads):
        part = slice(h * HD, h * HD + HD)
        pair = slice(128 * (h // 2), 128 * (h // 2) + 128)
        own = (lane >= HD) if h % 2 else (lane < HD)
        code = jnp.concatenate(
            [code_q_ref[: 2 * BITS].astype(f32)]
            + [piece.astype(f32) for piece in pieces(-lse_ref[0, h : h + 1, :])]
            + [jnp.zeros((HD - 2 * BITS - 3, rows), f32)],
            axis=0,
        ).astype(bf16)
        qt_ref[h] = other_half(turned[part], code, h)
        ka_ref[h] = jnp.where(own, keys[:, pair], code_k_ref[...])
        shift = jnp.concatenate(
            [piece.astype(f32) for piece in pieces(-delta[h : h + 1, :])]
            + [jnp.zeros((HD - 3, rows), f32)],
            axis=0,
        ).astype(bf16)
        dot_ref[h] = other_half(turned_grad[part], shift, h)
        va_ref[h] = jnp.where(own, values[:, pair], ones)
    dk_acc[...] = jnp.zeros_like(dk_acc)
    dv_acc[...] = jnp.zeros_like(dv_acc)

    def q_step(qi, _):
        q_rows = pl.ds(pl.multiple_of(qi * BACKWARD_TILE, BACKWARD_TILE), BACKWARD_TILE)
        low, high = key_range(ends, qi * BACKWARD_TILE, qi * BACKWARD_TILE + BACKWARD_TILE - 1, BACKWARD_TILE)
        dqt_ref[...] = jnp.zeros_like(dqt_ref)

        def k_step(ki, _):
            k_rows = pl.ds(pl.multiple_of(ki * BACKWARD_TILE, BACKWARD_TILE), BACKWARD_TILE)

            def products_of(h):
                return (
                    dot(ka_ref[h, k_rows, :], qt_ref[h, :, q_rows]),
                    dot(va_ref[h, k_rows, :], dot_ref[h, :, q_rows]),
                )

            ahead = [products_of(h) for h in range(2)]
            pending = []

            def finish(p, probs_a, grads_a, probs_b, grads_b):
                pair = slice(128 * p, 128 * p + 128)
                dv_acc[k_rows, pair] += dot(probs_a, dos_ref[2 * p, q_rows, :]) + dot(
                    probs_b, dos_ref[2 * p + 1, q_rows, :]
                )
                dk_acc[k_rows, pair] += dot(grads_a, qs_ref[2 * p, q_rows, :]) + dot(
                    grads_b, qs_ref[2 * p + 1, q_rows, :]
                )
                for h, grads in ((2 * p, grads_a), (2 * p + 1, grads_b)):
                    part = slice(h * HD, h * HD + HD)
                    dqt_ref[part, :] += dot(kt_ref[part, k_rows], grads)

            held = []
            for h in range(heads):
                if h + 2 < heads:
                    ahead.append(products_of(h + 2))
                scores, grad_probs = ahead[h]
                ahead[h] = None
                probs = jnp.exp(scores)
                grad_scores = (probs * grad_probs).astype(bf16)
                held += [probs.astype(bf16), grad_scores]
                if h % 2:
                    pending.append((h // 2, *held))
                    held = []
                if h % 2 and len(pending) > 1:
                    finish(*pending.pop(0))
            for item in pending:
                finish(*item)
            return 0

        lax.fori_loop(low, high, k_step, 0)
        dq_ref[q_rows, :] = (dqt_ref[...] * SCALE).T.astype(bf16)
        return 0

    lax.fori_loop(0, rows // BACKWARD_TILE, q_step, 0)
    dk_ref[...] = dk_acc[...].astype(bf16)
    dv_ref[...] = dv_acc[...].astype(bf16)
    for s, part in enumerate((dq_ref, dk_ref, dv_ref)):
        total_ref[...] = dot(xt_ref[...], part[...])
        store_blocks(place_ref, total_ref, near_ref, far_ref, (s,))
    gbias_ref[0:1, :] = jnp.sum(dq_ref[...].astype(f32), axis=0, keepdims=True)
    gbias_ref[1:2, :] = jnp.sum(dv_ref[...].astype(f32), axis=0, keepdims=True)


def attend_backward(group, lengths, place, tokens, query, keys, values, grad_mixed, mixed, lse):
    rows, width = tokens.shape
    cols = COLS
    heads = cols // HD
    size = width // BLOCKS
    by_group = pl.BlockSpec((rows, cols), lambda g: (0, group))
    own = pl.BlockSpec((rows, cols), lambda g: (0, 0))
    low = jax.ShapeDtypeStruct((rows, cols), bf16)
    return pl.pallas_call(
        attend_backward_kernel,
        grid=(1,),
        in_specs=[
            pl.BlockSpec(memory_space=pltpu.SMEM),
            pl.BlockSpec(memory_space=pltpu.SMEM),
            pl.BlockSpec((rows, width), lambda g: (0, 0)),
        ]
        + [own] * 3
        + [by_group]
        + [own]
        + [pl.BlockSpec((1, 8, rows), lambda g: (0, 0, 0))],
        out_specs=[own] * 3
        + [
            pl.BlockSpec((BLOCKS // 2, 3, size, cols), lambda g: (0, 0, 0, 0)),
            pl.BlockSpec((BLOCKS // 2, 3, size, cols), lambda g: (0, 0, 0, 0)),
            pl.BlockSpec((8, cols), lambda g: (0, 0)),
        ],
        out_shape=[low] * 3
        + [
            jax.ShapeDtypeStruct((BLOCKS // 2, 3, size, cols), bf16),
            jax.ShapeDtypeStruct((BLOCKS // 2, 3, size, cols), bf16),
            jax.ShapeDtypeStruct((8, cols), f32),
        ],
        scratch_shapes=[
            pltpu.VMEM((width, rows), bf16),
            pltpu.VMEM((heads, rows, 128), bf16),
            pltpu.VMEM((heads, rows, 128), bf16),
            pltpu.VMEM((heads, 128, rows), bf16),
            pltpu.VMEM((heads, 128, rows), bf16),
            pltpu.VMEM((heads, rows, 128), bf16),
            pltpu.VMEM((heads, rows, 128), bf16),
            pltpu.VMEM((cols, rows), bf16),
            pltpu.VMEM((HD, rows), bf16),
            pltpu.VMEM((rows, 128), bf16),
            pltpu.VMEM((cols, BACKWARD_TILE), f32),
            pltpu.VMEM((rows, cols), f32),
            pltpu.VMEM((rows, cols), f32),
            pltpu.VMEM((width, cols), f32),
        ],
        compiler_params=pltpu.CompilerParams(vmem_limit_bytes=44 << 20),
        cost_estimate=pl.CostEstimate(flops=12 * rows * width * width, bytes_accessed=16 << 20, transcendentals=0),
        name="attend_backward",
    )(lengths, place, tokens, query, keys, values, grad_mixed, mixed, lse)


def token_grad_kernel(gp_ref, *refs):
    *grads, w_ref, out_ref = refs
    total = gp_ref[...]
    cols = grads[0].shape[1]
    for i, grad in enumerate(grads):
        total = total + dot(grad[...], w_ref[:, i * cols : i * cols + cols], NT)
    out_ref[...] = total


def token_grad(grad_one, grads, full_qkv):
    rows, width = grad_one.shape
    cols = grads[0].shape[1]
    by_rows = pl.BlockSpec((TB, width), lambda i: (i, 0))
    return pl.pallas_call(
        token_grad_kernel,
        grid=(rows // TB,),
        in_specs=[by_rows]
        + [pl.BlockSpec((TB, cols), lambda i: (i, 0))] * len(grads)
        + [pl.BlockSpec((width, 3 * width), lambda i: (0, 0), pipeline_mode=pl.Buffered(1))],
        out_specs=by_rows,
        out_shape=jax.ShapeDtypeStruct((rows, width), f32),
        compiler_params=pltpu.CompilerParams(vmem_limit_bytes=28 << 20),
        cost_estimate=pl.CostEstimate(flops=6 * rows * width * width, bytes_accessed=14 << 20, transcendentals=0),
        name="token_grad",
    )(grad_one, *grads, full_qkv)


def assemble_kernel(blocks_ref, near_ref, far_ref, out_ref):
    count = near_ref.shape[0]
    for m in range(count):
        out_ref[blocks_ref[m]] = near_ref[m]
        out_ref[blocks_ref[count + m]] = far_ref[m]


def assemble(blocks_at, near, far):
    rows, cols = near.shape[1:]
    parts = 1
    while cols % (2 * parts * 128) == 0 and cols // parts > 1024:
        parts *= 2
    while cols // parts > 1024 and cols % (3 * parts * 128) == 0:
        parts *= 3
    by_cols = pl.BlockSpec((near.shape[0], rows, cols // parts), lambda i: (0, 0, i))
    return pl.pallas_call(
        assemble_kernel,
        grid=(parts,),
        in_specs=[pl.BlockSpec(memory_space=pltpu.SMEM), by_cols, by_cols],
        out_specs=pl.BlockSpec((BLOCKS, rows, cols // parts), lambda i: (0, 0, i)),
        out_shape=jax.ShapeDtypeStruct((BLOCKS, rows, cols), near.dtype),
        compiler_params=pltpu.CompilerParams(vmem_limit_bytes=20 << 20),
        cost_estimate=pl.CostEstimate(flops=0, bytes_accessed=4 * near.size * 2, transcendentals=0),
        name="assemble",
    )(blocks_at, near, far)


CORE, X, Y, Z_LOW, Z_HIGH = 1, 2, 4, 8, 16


def relative_places():
    places = np.zeros((32, 32), np.int32)
    for i in range(32):
        for b in range(32):
            bits = i ^ b
            x, y = int(bits & X > 0), int(bits & Y > 0)
            first, second = (y, x) if b & CORE else (x, y)
            low, high = int(bits & Z_LOW > 0), int(bits & Z_HIGH > 0)
            places[i, b] = 16 * (bits & CORE) + 8 * first + 4 * second + 2 * low + high
    return places


def exchange(values, even, odd):
    return lax.ppermute(
        values, "dp", [(i, i ^ (odd if i & CORE else even)) for i in range(32)]
    )


def added(a, b):
    return (a.astype(f32) + b.astype(f32)).astype(bf16)


def after(values, *earlier):
    return lax.optimization_barrier((values, *earlier))[0]


GATHER_HOPS = ((Z_HIGH, Z_HIGH), (Z_LOW, Z_LOW), (Y, X), (X, Y), (CORE, CORE))


def gather_blocks(*own):
    held = [part[None] for part in own]
    earlier = yield
    for hop in GATHER_HOPS:
        if earlier is not None:
            held[0] = after(held[0], *earlier)
        near, got = held[0], [exchange(part, *hop) for part in held]
        if hop[0] != CORE:
            held = [jnp.concatenate([jnp.concatenate(held, axis=2), jnp.concatenate(got, axis=2)], axis=0)]
        earlier = yield got[0], near


def fold(pairs):
    half = pairs[0][0].shape[0] // 2

    def joined(rows):
        return jnp.concatenate([added(kept[rows], got[rows]) for kept, got in pairs], axis=1)

    return joined(slice(half, 2 * half)), joined(slice(0, half))


def meet(parts):
    return [(near, exchange(far, CORE, CORE)) for near, far in parts]


def hop(state, even, odd):
    send, keep = state
    return keep, exchange(send, even, odd)


def total(pair):
    return pair[0][0].astype(f32) + pair[1][0].astype(f32)


def body(
    tokens, cotangent, lengths, w_qkv, w_out, w_up, w_down, bias_q, bias_v, bias_out,
    gain_one, shift_one, bias_up, bias_down, gain_two, shift_two,
):
    count = lax.axis_size("dp")
    index = lax.axis_index("dp")
    width = tokens.shape[1]
    units = w_up.shape[1]
    shard = w_qkv.shape[0]
    ratio = units // width
    small = jnp.concatenate(
        [bias_q, bias_v, bias_out, gain_one, shift_one, bias_down, gain_two, shift_two]
    )
    small = jnp.concatenate([small.reshape(8, shard).T, bias_up.reshape(shard, ratio)], axis=1)
    small = jnp.pad(small, ((0, 0), (0, 128 - small.shape[1])))
    up_out_shard = jnp.concatenate([w_up, w_out], axis=1)
    if count == BLOCKS:
        table = relative_places()
        core = np.arange(BLOCKS)[:, None] & CORE
        place = jnp.asarray(np.concatenate([table, core], axis=1).astype(np.int32))[index]
        blocks_at = jnp.asarray(np.argsort(table, axis=1).astype(np.int32))[index]
        first, second = gather_blocks(w_qkv, small), gather_blocks(up_out_shard)
        next(first)
        next(second)
        full_down = lax.all_gather(w_down, "dp", axis=0, tiled=True)
        hops = [first.send(None) for _ in range(5)]
        far, near = hops[4]
        full_qkv = assemble(blocks_at, near, far).reshape(width, -1)
        arrived = [second.send([hops[3][0]])[0], second.send([far])[0]]
    else:
        place = jnp.arange(BLOCKS, dtype=jnp.int32) // 2
        place = jnp.append(place, 0)
        full_qkv, full_up_out, full_down = (
            lax.all_gather(part, "dp", axis=0, tiled=True)
            for part in (jnp.concatenate([w_qkv, small], axis=1), up_out_shard, w_down)
        )
    vectors = full_qkv[:, 3 * width :]
    full_bias_up = vectors[:, 8 : 8 + ratio].reshape(1, units)

    forward = []
    for g in range(width // COLS):
        held = tokens
        if count == BLOCKS:
            held = after(tokens, arrived[g])
            if g:
                arrived.append(second.send([forward[-1][3]])[0])
        forward.append(attend_forward(g, lengths, held, full_qkv))
    if count == BLOCKS:
        far, near = second.send([part[3] for part in forward])
        full_up_out = assemble(blocks_at, near, far).reshape(width, -1)
    (
        output, grad_one, grad_attn, grad_mixed, hidden_low, grad_branch, mixed, active, grad_up,
        gvec, gbu,
    ) = feed_forward(
        lengths, tokens, [part[3] for part in forward], cotangent, full_up_out, full_down,
        full_qkv, full_bias_up,
    )
    part_down = weight_grad_tall(place, active, grad_branch)
    part_up = weight_grad_wide(place, after(hidden_low, part_down[0]), grad_up, width)
    part_out = weight_grad_wide(place, after(mixed, part_up[0]), grad_attn, COLS)
    milestones = []

    def backward(g):
        held = after(grad_mixed, *milestones)
        query, keys, values, own_mixed, lse = forward[g]
        return attend_backward(g, lengths, place, tokens, query, keys, values, held, own_mixed, lse)

    if count != BLOCKS:
        groups = [backward(g) for g in range(width // COLS)]
        grad_tokens = token_grad(
            grad_one, [group[s] for s in range(3) for group in groups], full_qkv
        )
        gbias = jnp.concatenate([group[5] for group in groups], axis=1)
        def scattered(part):
            return lax.psum_scatter(part, "dp", scatter_dimension=0, tiled=True).astype(f32)

        def lined(halves):
            part = jnp.stack(halves, axis=1).reshape(BLOCKS, *halves[0].shape[1:])
            return part.transpose(0, 2, 1, 3).reshape(width, -1)

        part_qkv = [jnp.concatenate([group[h] for group in groups], axis=3) for h in (3, 4)]
        tall_down = jnp.stack(part_down, axis=1).reshape(units, width)
        return (
            output, grad_tokens, scattered(lined(part_qkv)), scattered(lined(part_out)),
            scattered(lined(part_up)), scattered(tall_down),
            scattered(gbias[0]), scattered(gbias[1]), scattered(gvec[5]), scattered(gvec[3]),
            scattered(gvec[4]), scattered(gbu[0]), scattered(gvec[2]), scattered(gvec[0]),
            scattered(gvec[1]),
        )

    def small_part(lines, width):
        line = jnp.concatenate(
            [
                part.reshape(part.shape[0], BLOCKS, -1).transpose(1, 0, 2).reshape(BLOCKS, -1)
                for part in lines
            ],
            axis=1,
        )
        line = jnp.pad(line.astype(bf16), ((0, 0), (0, width - line.shape[1])))
        line = jnp.pad(line[blocks_at][:, None, :], ((0, 0), (0, 7), (0, 0)))
        return line[: BLOCKS // 2], line[BLOCKS // 2 :]

    def rows_of(halves):
        return [half.reshape(half.shape[0], -1, half.shape[-1]) for half in halves]

    small_mlp = small_part([gvec[:6], gbu], width)
    down = fold(meet([part_down, small_mlp]))
    down_first = hop(down, X, Y)
    up_met = meet([rows_of(part_up)])
    out_met = meet([rows_of(part_out)])
    up = fold(up_met)
    milestones += [part_out[0], up[0]]
    groups = [backward(0)]
    up_first = hop(up, X, Y)
    milestones[:] = [groups[0][0]]
    mlp = fold([down_first, up_first])
    milestones += [mlp[0]]
    groups.append(backward(1))
    mlp = fold([hop(mlp, Y, X)])
    early = fold(out_met + meet([rows_of(groups[0][3:5])]))
    milestones[:] = [groups[1][0], mlp[0], early[0]]
    groups.append(backward(2))
    mlp = fold([hop(mlp, Z_LOW, Z_LOW)])
    early_first = hop(early, X, Y)
    gbias = jnp.concatenate([group[5] for group in groups], axis=1)
    small_attn = small_part([gbias[:2]], COLS)
    late = fold(meet([rows_of(groups[1][3:5]), rows_of(groups[2][3:5]), small_attn]))
    late_first = hop(late, X, Y)
    grad_tokens = token_grad(
        grad_one, [group[s] for s in range(3) for group in groups], full_qkv
    )
    mlp = total(hop(mlp, Z_HIGH, Z_HIGH))
    attn = fold([early_first, late_first])
    attn = fold([hop(attn, Y, X)])
    attn = fold([hop(attn, Z_LOW, Z_LOW)])
    attn = total(hop(attn, Z_HIGH, Z_HIGH))

    def wide_of(rows):
        return rows.reshape(-1, shard, width).transpose(1, 0, 2).reshape(shard, -1)

    tall = ratio * shard
    line = mlp[tall]
    attn = [attn[i * shard : i * shard + shard] for i in range(12)] + [attn[12 * shard]]
    line_attn = attn[12]
    grad_out_weight = jnp.concatenate(attn[:3], axis=1)
    grad_qkv = jnp.concatenate([attn[3 + 3 * g + s] for s in range(3) for g in range(3)], axis=1)

    def piece(line, i):
        return line[i * shard : i * shard + shard]

    return (
        output, grad_tokens, grad_qkv, grad_out_weight,
        wide_of(mlp[tall + 8 :]), mlp[:tall],
        piece(line_attn, 0), piece(line_attn, 1), piece(line, 5), piece(line, 3), piece(line, 4),
        line[6 * shard : 6 * shard + tall], piece(line, 2), piece(line, 0), piece(line, 1),
    )


def solution(mesh):
    rows, vector = P("dp", None), P("dp")
    return jax.shard_map(
        body, mesh=mesh, in_specs=(rows,) * 7 + (vector,) * 9, out_specs=(rows,) * 6 + (vector,) * 9,
        check_vma=False,
    )
```

```python
import functools
import math

import jax
import jax.numpy as jnp
import numpy as np
from jax import lax
from jax.experimental import pallas as pl
from jax.experimental.pallas import tpu as pltpu
from jax.sharding import PartitionSpec as P

HD = 64
FORWARD_TILE = 512
BACKWARD_TILE = 256
FAR = 2.0**30
BITS = 11
COLS = 256
TB = 256
FB = 768
BLOCKS = 32
NORM_EPS = 1e-06
SCALE = 1.0 / math.sqrt(HD)
NT = (((1,), (1,)), ((), ()))
TN = (((0,), (0,)), ((), ()))
f32 = jnp.float32
bf16 = jnp.bfloat16


def dot(a, b, dims=(((1,), (0,)), ((), ()))):
    return lax.dot_general(a, b, dims, preferred_element_type=f32)


def ends_of(len_ref):
    ends, total = [], jnp.int32(0)
    for j in range(len_ref.shape[1]):
        total = total + len_ref[0, j]
        ends.append(total)
    return ends


def segment_of(position, ends):
    member = jnp.zeros_like(position)
    for end in ends:
        member = member + (position >= end).astype(jnp.int32)
    return jnp.where(position < ends[-1], member, position + len(ends))


def key_range(ends, first, last, tile):
    low, high = jnp.int32(0), jnp.int32(0)
    start = jnp.int32(0)
    for end in ends:
        low = jnp.where((first >= start) & (first < end), start, low)
        high = jnp.where((last >= start) & (last < end), end, high)
        start = end
    total = ends[-1]
    low = jnp.where(first >= total, first, low)
    high = jnp.where(last >= total, last + 1, high)
    return low // tile, (high + tile - 1) // tile


def other_half(own, other, h):
    return jnp.concatenate([other, own] if h % 2 else [own, other], axis=0)


def segment_codes(rows, ends):
    spot = lax.broadcasted_iota(jnp.int32, (HD, rows), 0)
    seg = segment_of(lax.broadcasted_iota(jnp.int32, (1, rows), 1), ends)
    bit = (seg >> (spot // 2)) & 1
    code_q = jnp.where(spot < 2 * BITS, jnp.where(spot % 2 == 0, bit, 1 - bit), 0)
    spot = lax.broadcasted_iota(jnp.int32, (rows, 128), 1) % HD
    seg = segment_of(lax.broadcasted_iota(jnp.int32, (rows, 128), 0), ends)
    bit = (seg >> (spot // 2)) & 1
    code_k = jnp.where(spot < 2 * BITS, jnp.where(spot % 2 == 0, 1 - bit, bit), 0)
    return code_q.astype(f32).astype(bf16), code_k.astype(f32) * -FAR


def pieces(value):
    high = value.astype(bf16)
    rest = value - high.astype(f32)
    middle = rest.astype(bf16)
    return [high, middle, (rest - middle.astype(f32)).astype(bf16)]


def attend_forward_kernel(
    group, len_ref, x_ref, wq_ref, wk_ref, wv_ref, vec_ref,
    q_ref, k_ref, v_ref, mixed_ref, lse_ref,
    qt_ref, ka_ref, vt_ref, code_q_ref, code_k_ref, acc_ref, top_ref, bias_ref,
):
    ends = ends_of(len_ref)

    code_q_ref[...], code_k = segment_codes(q_ref.shape[0], ends)
    code_k_ref[...] = code_k.astype(bf16)
    bias_ref[...] = vec_ref[...].astype(f32).T[:8]

    rows, cols = q_ref.shape
    heads = cols // HD
    own_cols = slice(group * cols, group * cols + cols)
    x = x_ref[...]
    query = (dot(x, wq_ref[...]) + bias_ref[0:1, own_cols]).astype(bf16)
    q_ref[...] = query
    keys = dot(x, wk_ref[...]).astype(bf16)
    k_ref[...] = keys
    value = (dot(x, wv_ref[...]) + bias_ref[1:2, own_cols]).astype(bf16)
    v_ref[...] = value
    turned, turned_value = (query * bf16(SCALE)).T, value.T
    lane = lax.broadcasted_iota(jnp.int32, (rows, 128), 1)
    for h in range(heads):
        part = slice(h * HD, h * HD + HD)
        own = (lane >= HD) if h % 2 else (lane < HD)
        qt_ref[h] = other_half(turned[part], code_q_ref[...], h)
        ka_ref[h] = jnp.where(own, keys[:, 128 * (h // 2) : 128 * (h // 2) + 128], code_k_ref[...])
        vt_ref[h, :HD] = turned_value[part]
        vt_ref[h, HD:] = jnp.ones((16, rows), bf16)

    def q_step(qi, _):
        q_cols = pl.ds(pl.multiple_of(qi * FORWARD_TILE, FORWARD_TILE), FORWARD_TILE)
        low, high = key_range(ends, qi * FORWARD_TILE, qi * FORWARD_TILE + FORWARD_TILE - 1, FORWARD_TILE)
        acc_ref[...] = jnp.zeros_like(acc_ref)
        top_ref[...] = jnp.full_like(top_ref, -3e38)

        def k_step(ki, _):
            k_rows = pl.ds(pl.multiple_of(ki * FORWARD_TILE, FORWARD_TILE), FORWARD_TILE)
            tops = top_ref[...]
            new_tops = []

            def scores_of(h):
                return dot(ka_ref[h, k_rows, :], qt_ref[h, :, q_cols])

            ahead = [scores_of(h) for h in range(1)]
            pending = []

            def finish(h, low_weights, fade):
                acc_ref[h] = acc_ref[h] * fade + dot(vt_ref[h, :, k_rows], low_weights)

            for h in range(heads):
                if h + 1 < heads:
                    ahead.append(scores_of(h + 1))
                scores = ahead[h]
                ahead[h] = None
                before = tops[h : h + 1]
                top = jnp.maximum(before, jnp.max(scores, axis=0, keepdims=True))
                new_tops.append(top)
                pending.append((h, jnp.exp(scores - top).astype(bf16), jnp.exp(before - top)))
                if len(pending) > 0:
                    finish(*pending.pop(0))
            for item in pending:
                finish(*item)
            spare = [jnp.zeros((8 - heads, FORWARD_TILE), f32)]
            top_ref[...] = jnp.concatenate(new_tops + spare, axis=0)
            return 0

        lax.fori_loop(low, high, k_step, 0)
        totals = jnp.concatenate([acc_ref[h, HD : HD + 1] for h in range(heads)], axis=0)
        for p in range(heads // 2):
            halves = [acc_ref[h, :HD] / totals[h : h + 1] for h in (2 * p, 2 * p + 1)]
            mixed = jnp.concatenate(halves, axis=0)
            mixed_ref[q_cols, 128 * p : 128 * p + 128] = mixed.T.astype(bf16)
        lse = top_ref[0:heads] + jnp.log(totals)
        lse_ref[0, :, q_cols] = jnp.concatenate([lse, jnp.zeros((8 - heads, FORWARD_TILE), f32)], axis=0)
        return 0

    lax.fori_loop(0, rows // FORWARD_TILE, q_step, 0)


def attend_forward(group, lengths, tokens, full_qkv):
    rows, width = tokens.shape
    cols = COLS
    groups = width // cols
    heads = cols // HD
    low = jax.ShapeDtypeStruct((rows, cols), bf16)
    own = pl.BlockSpec((rows, cols), lambda g: (0, 0))
    return pl.pallas_call(
        functools.partial(attend_forward_kernel, group),
        grid=(1,),
        in_specs=[
            pl.BlockSpec(memory_space=pltpu.SMEM),
            pl.BlockSpec((rows, width), lambda g: (0, 0)),
            pl.BlockSpec((width, cols), lambda g: (0, group)),
            pl.BlockSpec((width, cols), lambda g: (0, group + groups)),
            pl.BlockSpec((width, cols), lambda g: (0, group + 2 * groups)),
            pl.BlockSpec((width, 128), lambda g: (0, 3 * width // 128)),
        ],
        out_specs=[own] * 4 + [pl.BlockSpec((1, 8, rows), lambda g: (0, 0, 0))],
        out_shape=[low] * 4 + [jax.ShapeDtypeStruct((1, 8, rows), f32)],
        scratch_shapes=[
            pltpu.VMEM((heads, 128, rows), bf16),
            pltpu.VMEM((heads, rows, 128), bf16),
            pltpu.VMEM((heads, HD + 16, rows), bf16),
            pltpu.VMEM((HD, rows), bf16),
            pltpu.VMEM((rows, 128), bf16),
            pltpu.VMEM((heads, HD + 16, FORWARD_TILE), f32),
            pltpu.VMEM((8, FORWARD_TILE), f32),
            pltpu.VMEM((8, width), f32),
        ],
        compiler_params=pltpu.CompilerParams(vmem_limit_bytes=60 << 20),
        cost_estimate=pl.CostEstimate(flops=12 * rows * width * width, bytes_accessed=12 << 20, transcendentals=0),
        name="attend_forward",
    )(lengths, tokens, full_qkv, full_qkv, full_qkv, full_qkv)


def feed_forward_kernel(
    len_ref, x_ref, mixed_a_ref, mixed_b_ref, mixed_c_ref, cot_ref, wo_ref, wu_ref, wd_ref, vec_ref, bu_ref,
    out_ref, gp_ref, ga_ref, gm_ref, hl_ref, gb_ref, mixed_ref, act_ref, gu_ref, gvec_ref, gbu_ref,
    slope_ref, rows_ref,
):
    step = pl.program_id(0)
    rows, width = x_ref.shape
    hidden_units = bu_ref.shape[1]

    @pl.when(step == 0)
    def _():
        gvec_ref[...] = jnp.zeros_like(gvec_ref)
        gbu_ref[...] = jnp.zeros_like(gbu_ref)
        rows_ref[...] = vec_ref[...].astype(f32).T[:8]

    total = ends_of(len_ref)[-1]
    position = step * rows + lax.broadcasted_iota(jnp.int32, (rows, 1), 0)
    valid = (position < total).astype(f32)

    def vec(i):
        return rows_ref[i + 2 : i + 3, :]

    def norm(values):
        centered = values - jnp.mean(values, axis=1, keepdims=True)
        scale = lax.rsqrt(jnp.mean(centered * centered, axis=1, keepdims=True) + NORM_EPS)
        return centered * scale, scale

    def norm_back(grad, gain, unit, scale):
        grad = grad * gain
        mean_grad = jnp.mean(grad, axis=1, keepdims=True)
        mean_unit = jnp.mean(grad * unit, axis=1, keepdims=True)
        return scale * (grad - mean_grad - unit * mean_unit)

    def add_vec(i, value):
        gvec_ref[i : i + 1, :] += jnp.sum(value, axis=0, keepdims=True)

    mixed_ref[...] = jnp.concatenate(
        [mixed_a_ref[...], mixed_b_ref[...], mixed_c_ref[...]], axis=1
    )
    pre_one = x_ref[...].astype(f32) + dot(mixed_ref[...], wo_ref[...]) + vec(0)
    unit_one, scale_one = norm(pre_one)
    hidden = unit_one * vec(1) + vec(2)
    hidden_low = hidden.astype(bf16)
    hl_ref[...] = hidden_low
    branch = jnp.zeros((rows, width), f32)
    parts = [slice(f * FB, f * FB + FB) for f in range(hidden_units // FB)]
    ahead = dot(hidden_low, wu_ref[:, parts[0]])
    for f, part in enumerate(parts):
        up = ahead + bu_ref[:, part].astype(f32)
        if f + 1 < len(parts):
            ahead = dot(hidden_low, wu_ref[:, parts[f + 1]])
        bell = jnp.exp(up * up * -0.5)
        t = 1.0 / (1.0 + (0.3275911 * math.sqrt(0.5)) * jnp.abs(up))
        poly = 0.5 * 1.061405429 * t - 0.5 * 1.453152027
        poly = poly * t + 0.5 * 1.421413741
        poly = poly * t - 0.5 * 0.284496736
        poly = poly * t + 0.5 * 0.254829592
        tail = poly * t * bell
        share = jnp.where(up >= 0, 1.0 - tail, tail)
        active = (up * share).astype(bf16)
        act_ref[:, part] = active
        slope_ref[:, part] = share + up * bell * (1.0 / math.sqrt(2.0 * math.pi))
        branch = branch + dot(active, wd_ref[part, :])
    unit_two, scale_two = norm(hidden + branch + vec(3))
    out_ref[...] = (valid * (unit_two * vec(4) + vec(5))).astype(bf16)
    grad_out = valid * cot_ref[...].astype(f32)
    add_vec(0, grad_out * unit_two)
    add_vec(1, grad_out)
    grad_two = norm_back(grad_out, vec(4), unit_two, scale_two)
    grad_branch = grad_two.astype(bf16)
    gb_ref[...] = grad_branch
    add_vec(2, grad_branch.astype(f32))
    grad_hidden = grad_two
    ahead = dot(grad_branch, wd_ref[parts[0], :], NT)
    for f, part in enumerate(parts):
        grad_up = (ahead * slope_ref[:, part]).astype(bf16)
        if f + 1 < len(parts):
            ahead = dot(grad_branch, wd_ref[parts[f + 1], :], NT)
        gu_ref[:, part] = grad_up
        gbu_ref[:, part] += jnp.sum(grad_up.astype(f32), axis=0, keepdims=True)
        grad_hidden = grad_hidden + dot(grad_up, wu_ref[:, part], NT)
    add_vec(3, grad_hidden * unit_one)
    add_vec(4, grad_hidden)
    grad_one = norm_back(grad_hidden, vec(1), unit_one, scale_one)
    gp_ref[...] = grad_one
    grad_attn = grad_one.astype(bf16)
    ga_ref[...] = grad_attn
    add_vec(5, grad_attn.astype(f32))
    gm_ref[...] = dot(grad_attn, wo_ref[...], NT).astype(bf16)


def feed_forward(lengths, tokens, mixed, cotangent, full_up_out, full_down, full_qkv, bias_up):
    rows, width = tokens.shape
    units = bias_up.shape[1]
    by_rows = pl.BlockSpec((TB, width), lambda i: (i, 0))
    by_units = pl.BlockSpec((TB, units), lambda i: (i, 0))

    def whole(shape, column=0):
        return pl.BlockSpec(shape, lambda i: (0, column), pipeline_mode=pl.Buffered(1))

    def kept(shape):
        return pl.BlockSpec(shape, lambda i: (0,) * len(shape))

    low = jax.ShapeDtypeStruct((rows, width), bf16)
    wide = jax.ShapeDtypeStruct((rows, units), bf16)
    return pl.pallas_call(
        feed_forward_kernel,
        grid=(rows // TB,),
        in_specs=[
            pl.BlockSpec(memory_space=pltpu.SMEM),
            by_rows, *[pl.BlockSpec((TB, part.shape[1]), lambda i: (i, 0)) for part in mixed], by_rows,
            whole((width, width), units // width), whole((width, units)), whole(full_down.shape),
            whole((width, 128), 3 * width // 128), whole(bias_up.shape),
        ],
        out_specs=[by_rows] * 7 + [by_units] * 2 + [kept((8, width)), kept((1, units))],
        out_shape=[low, jax.ShapeDtypeStruct((rows, width), f32), low, low, low, low, low, wide, wide,
                   jax.ShapeDtypeStruct((8, width), f32), jax.ShapeDtypeStruct((1, units), f32)],
        scratch_shapes=[pltpu.VMEM((TB, units), f32), pltpu.VMEM((8, width), f32)],
        compiler_params=pltpu.CompilerParams(vmem_limit_bytes=56 << 20),
        cost_estimate=pl.CostEstimate(flops=8 * rows * width * units + 4 * rows * width * width, bytes_accessed=40 << 20, transcendentals=0),
        name="feed_forward",
    )(lengths, tokens, *mixed, cotangent, full_up_out, full_up_out, full_down, full_qkv, bias_up)


def store_blocks(place_ref, total_ref, near_ref, far_ref, at, base=0):
    size = near_ref.shape[-2]
    own = place_ref[BLOCKS]
    for pair in range(total_ref.shape[0] // (2 * size)):
        for ref, core in ((near_ref, own), (far_ref, 1 - own)):
            block = 2 * pair + core
            rows = pl.ds(pl.multiple_of(block * size, size), size)
            ref[(place_ref[base + block] % (BLOCKS // 2), *at)] = total_ref[rows, :].astype(bf16)


def weight_grad_kernel(place_ref, left_ref, right_ref, near_ref, far_ref, left_t_ref, total_ref):
    @pl.when(pl.program_id(0) == 0)
    def _():
        left_t_ref[...] = left_ref[...].T

    total_ref[...] = dot(left_t_ref[...], right_ref[...])
    store_blocks(place_ref, total_ref, near_ref, far_ref, (0,))


def weight_grad_wide(place, left, right, cols):
    rows, width = left.shape
    groups = right.shape[1] // cols
    size = width // BLOCKS
    return pl.pallas_call(
        weight_grad_kernel,
        grid=(groups,),
        in_specs=[
            pl.BlockSpec(memory_space=pltpu.SMEM),
            pl.BlockSpec((rows, width), lambda g: (0, 0)),
            pl.BlockSpec((rows, cols), lambda g: (0, g)),
        ],
        out_specs=[pl.BlockSpec((BLOCKS // 2, 1, size, cols), lambda g: (0, g, 0, 0))] * 2,
        out_shape=[jax.ShapeDtypeStruct((BLOCKS // 2, groups, size, cols), bf16)] * 2,
        scratch_shapes=[pltpu.VMEM((width, rows), bf16), pltpu.VMEM((width, cols), f32)],
        compiler_params=pltpu.CompilerParams(vmem_limit_bytes=20 << 20),
        cost_estimate=pl.CostEstimate(flops=2 * rows * width * right.shape[1], bytes_accessed=12 << 20, transcendentals=0),
        name="weight_grad_wide",
    )(place, left, right)


def weight_grad_tall_kernel(place_ref, left_ref, right_ref, near_ref, far_ref, total_ref):
    total_ref[...] = dot(left_ref[...], right_ref[...], TN)
    base = pl.program_id(0) * (total_ref.shape[0] // near_ref.shape[1])
    store_blocks(place_ref, total_ref, near_ref, far_ref, (), base)


def weight_grad_tall(place, left, right):
    rows, units = left.shape
    width = right.shape[1]
    size = units // BLOCKS
    return pl.pallas_call(
        weight_grad_tall_kernel,
        grid=(units // width,),
        in_specs=[
            pl.BlockSpec(memory_space=pltpu.SMEM),
            pl.BlockSpec((rows, width), lambda g: (0, g)),
            pl.BlockSpec((rows, width), lambda g: (0, 0)),
        ],
        out_specs=[pl.BlockSpec((BLOCKS // 2, size, width), lambda g: (0, 0, 0))] * 2,
        out_shape=[jax.ShapeDtypeStruct((BLOCKS // 2, size, width), bf16)] * 2,
        scratch_shapes=[pltpu.VMEM((width, width), f32)],
        compiler_params=pltpu.CompilerParams(vmem_limit_bytes=20 << 20),
        cost_estimate=pl.CostEstimate(flops=2 * rows * width * units, bytes_accessed=12 << 20, transcendentals=0),
        name="weight_grad_tall",
    )(place, left, right)


def attend_backward_kernel(
    len_ref, place_ref, x_ref, q_ref, k_ref, v_ref, do_ref, o_ref, lse_ref,
    dq_ref, dk_ref, dv_ref, near_ref, far_ref, gbias_ref,
    xt_ref, qs_ref, dos_ref, qt_ref, dot_ref, ka_ref, va_ref, kt_ref, code_q_ref, code_k_ref,
    dqt_ref, dk_acc, dv_acc, total_ref,
):
    rows, cols = q_ref.shape
    heads = cols // HD
    ends = ends_of(len_ref)

    xt_ref[...] = x_ref[...].T
    code_q, code_k = segment_codes(rows, ends)
    code_q_ref[...] = code_q
    spot = lax.broadcasted_iota(jnp.int32, (rows, 128), 1) % HD
    code_k_ref[...] = jnp.where((spot >= 2 * BITS) & (spot < 2 * BITS + 3), 1.0, code_k).astype(bf16)

    query, keys, values, grad = q_ref[...], k_ref[...], v_ref[...], do_ref[...]
    lane = lax.broadcasted_iota(jnp.int32, (rows, 128), 1)
    for h in range(heads):
        pair = slice(128 * (h // 2), 128 * (h // 2) + 128)
        own = (lane >= HD) if h % 2 else (lane < HD)
        qs_ref[h] = jnp.where(own, query[:, pair] * bf16(SCALE), bf16(0))
        dos_ref[h] = jnp.where(own, grad[:, pair], bf16(0))
    kt_ref[...] = keys.T
    product = grad.astype(f32) * o_ref[...].astype(f32)
    high_part = product.astype(bf16)
    low_part = (product - high_part.astype(f32)).astype(bf16)
    pick = (
        lax.broadcasted_iota(jnp.int32, (8, cols), 1) // HD
        == lax.broadcasted_iota(jnp.int32, (8, cols), 0)
    ).astype(bf16)
    delta = dot(pick, high_part, NT) + dot(pick, low_part, NT)
    turned, turned_grad = (query * bf16(SCALE)).T, grad.T
    lane = lax.broadcasted_iota(jnp.int32, (rows, 128), 1)
    ones = jnp.where(lane % HD < 3, 1.0, 0.0).astype(bf16)
    for h in range(heads):
        part = slice(h * HD, h * HD + HD)
        pair = slice(128 * (h // 2), 128 * (h // 2) + 128)
        own = (lane >= HD) if h % 2 else (lane < HD)
        code = jnp.concatenate(
            [code_q_ref[: 2 * BITS].astype(f32)]
            + [piece.astype(f32) for piece in pieces(-lse_ref[0, h : h + 1, :])]
            + [jnp.zeros((HD - 2 * BITS - 3, rows), f32)],
            axis=0,
        ).astype(bf16)
        qt_ref[h] = other_half(turned[part], code, h)
        ka_ref[h] = jnp.where(own, keys[:, pair], code_k_ref[...])
        shift = jnp.concatenate(
            [piece.astype(f32) for piece in pieces(-delta[h : h + 1, :])]
            + [jnp.zeros((HD - 3, rows), f32)],
            axis=0,
        ).astype(bf16)
        dot_ref[h] = other_half(turned_grad[part], shift, h)
        va_ref[h] = jnp.where(own, values[:, pair], ones)
    dk_acc[...] = jnp.zeros_like(dk_acc)
    dv_acc[...] = jnp.zeros_like(dv_acc)

    def q_step(qi, _):
        q_rows = pl.ds(pl.multiple_of(qi * BACKWARD_TILE, BACKWARD_TILE), BACKWARD_TILE)
        low, high = key_range(ends, qi * BACKWARD_TILE, qi * BACKWARD_TILE + BACKWARD_TILE - 1, BACKWARD_TILE)
        dqt_ref[...] = jnp.zeros_like(dqt_ref)

        def k_step(ki, _):
            k_rows = pl.ds(pl.multiple_of(ki * BACKWARD_TILE, BACKWARD_TILE), BACKWARD_TILE)

            def products_of(h):
                return (
                    dot(ka_ref[h, k_rows, :], qt_ref[h, :, q_rows]),
                    dot(va_ref[h, k_rows, :], dot_ref[h, :, q_rows]),
                )

            ahead = [products_of(h) for h in range(2)]
            pending = []

            def finish(p, probs_a, grads_a, probs_b, grads_b):
                pair = slice(128 * p, 128 * p + 128)
                dv_acc[k_rows, pair] += dot(probs_a, dos_ref[2 * p, q_rows, :]) + dot(
                    probs_b, dos_ref[2 * p + 1, q_rows, :]
                )
                dk_acc[k_rows, pair] += dot(grads_a, qs_ref[2 * p, q_rows, :]) + dot(
                    grads_b, qs_ref[2 * p + 1, q_rows, :]
                )
                for h, grads in ((2 * p, grads_a), (2 * p + 1, grads_b)):
                    part = slice(h * HD, h * HD + HD)
                    dqt_ref[part, :] += dot(kt_ref[part, k_rows], grads)

            held = []
            for h in range(heads):
                if h + 2 < heads:
                    ahead.append(products_of(h + 2))
                scores, grad_probs = ahead[h]
                ahead[h] = None
                probs = jnp.exp(scores)
                grad_scores = (probs * grad_probs).astype(bf16)
                held += [probs.astype(bf16), grad_scores]
                if h % 2:
                    pending.append((h // 2, *held))
                    held = []
                if h % 2 and len(pending) > 1:
                    finish(*pending.pop(0))
            for item in pending:
                finish(*item)
            return 0

        lax.fori_loop(low, high, k_step, 0)
        dq_ref[q_rows, :] = (dqt_ref[...] * SCALE).T.astype(bf16)
        return 0

    lax.fori_loop(0, rows // BACKWARD_TILE, q_step, 0)
    dk_ref[...] = dk_acc[...].astype(bf16)
    dv_ref[...] = dv_acc[...].astype(bf16)
    for s, part in enumerate((dq_ref, dk_ref, dv_ref)):
        total_ref[...] = dot(xt_ref[...], part[...])
        store_blocks(place_ref, total_ref, near_ref, far_ref, (s,))
    gbias_ref[0:1, :] = jnp.sum(dq_ref[...].astype(f32), axis=0, keepdims=True)
    gbias_ref[1:2, :] = jnp.sum(dv_ref[...].astype(f32), axis=0, keepdims=True)


def attend_backward(group, lengths, place, tokens, query, keys, values, grad_mixed, mixed, lse):
    rows, width = tokens.shape
    cols = COLS
    heads = cols // HD
    size = width // BLOCKS
    by_group = pl.BlockSpec((rows, cols), lambda g: (0, group))
    own = pl.BlockSpec((rows, cols), lambda g: (0, 0))
    low = jax.ShapeDtypeStruct((rows, cols), bf16)
    return pl.pallas_call(
        attend_backward_kernel,
        grid=(1,),
        in_specs=[
            pl.BlockSpec(memory_space=pltpu.SMEM),
            pl.BlockSpec(memory_space=pltpu.SMEM),
            pl.BlockSpec((rows, width), lambda g: (0, 0)),
        ]
        + [own] * 3
        + [by_group]
        + [own]
        + [pl.BlockSpec((1, 8, rows), lambda g: (0, 0, 0))],
        out_specs=[own] * 3
        + [
            pl.BlockSpec((BLOCKS // 2, 3, size, cols), lambda g: (0, 0, 0, 0)),
            pl.BlockSpec((BLOCKS // 2, 3, size, cols), lambda g: (0, 0, 0, 0)),
            pl.BlockSpec((8, cols), lambda g: (0, 0)),
        ],
        out_shape=[low] * 3
        + [
            jax.ShapeDtypeStruct((BLOCKS // 2, 3, size, cols), bf16),
            jax.ShapeDtypeStruct((BLOCKS // 2, 3, size, cols), bf16),
            jax.ShapeDtypeStruct((8, cols), f32),
        ],
        scratch_shapes=[
            pltpu.VMEM((width, rows), bf16),
            pltpu.VMEM((heads, rows, 128), bf16),
            pltpu.VMEM((heads, rows, 128), bf16),
            pltpu.VMEM((heads, 128, rows), bf16),
            pltpu.VMEM((heads, 128, rows), bf16),
            pltpu.VMEM((heads, rows, 128), bf16),
            pltpu.VMEM((heads, rows, 128), bf16),
            pltpu.VMEM((cols, rows), bf16),
            pltpu.VMEM((HD, rows), bf16),
            pltpu.VMEM((rows, 128), bf16),
            pltpu.VMEM((cols, BACKWARD_TILE), f32),
            pltpu.VMEM((rows, cols), f32),
            pltpu.VMEM((rows, cols), f32),
            pltpu.VMEM((width, cols), f32),
        ],
        compiler_params=pltpu.CompilerParams(vmem_limit_bytes=44 << 20),
        cost_estimate=pl.CostEstimate(flops=12 * rows * width * width, bytes_accessed=16 << 20, transcendentals=0),
        name="attend_backward",
    )(lengths, place, tokens, query, keys, values, grad_mixed, mixed, lse)


def token_grad_kernel(gp_ref, *refs):
    *grads, w_ref, out_ref = refs
    total = gp_ref[...]
    cols = grads[0].shape[1]
    for i, grad in enumerate(grads):
        total = total + dot(grad[...], w_ref[:, i * cols : i * cols + cols], NT)
    out_ref[...] = total


def token_grad(grad_one, grads, full_qkv):
    rows, width = grad_one.shape
    cols = grads[0].shape[1]
    by_rows = pl.BlockSpec((TB, width), lambda i: (i, 0))
    return pl.pallas_call(
        token_grad_kernel,
        grid=(rows // TB,),
        in_specs=[by_rows]
        + [pl.BlockSpec((TB, cols), lambda i: (i, 0))] * len(grads)
        + [pl.BlockSpec((width, 3 * width), lambda i: (0, 0), pipeline_mode=pl.Buffered(1))],
        out_specs=by_rows,
        out_shape=jax.ShapeDtypeStruct((rows, width), f32),
        compiler_params=pltpu.CompilerParams(vmem_limit_bytes=28 << 20),
        cost_estimate=pl.CostEstimate(flops=6 * rows * width * width, bytes_accessed=14 << 20, transcendentals=0),
        name="token_grad",
    )(grad_one, *grads, full_qkv)


def assemble_kernel(blocks_ref, near_ref, far_ref, out_ref):
    count = near_ref.shape[0]
    for m in range(count):
        out_ref[blocks_ref[m]] = near_ref[m]
        out_ref[blocks_ref[count + m]] = far_ref[m]


def assemble(blocks_at, near, far):
    rows, cols = near.shape[1:]
    parts = 1
    while cols % (2 * parts * 128) == 0 and cols // parts > 1024:
        parts *= 2
    while cols // parts > 1024 and cols % (3 * parts * 128) == 0:
        parts *= 3
    by_cols = pl.BlockSpec((near.shape[0], rows, cols // parts), lambda i: (0, 0, i))
    return pl.pallas_call(
        assemble_kernel,
        grid=(parts,),
        in_specs=[pl.BlockSpec(memory_space=pltpu.SMEM), by_cols, by_cols],
        out_specs=pl.BlockSpec((BLOCKS, rows, cols // parts), lambda i: (0, 0, i)),
        out_shape=jax.ShapeDtypeStruct((BLOCKS, rows, cols), near.dtype),
        compiler_params=pltpu.CompilerParams(vmem_limit_bytes=20 << 20),
        cost_estimate=pl.CostEstimate(flops=0, bytes_accessed=4 * near.size * 2, transcendentals=0),
        name="assemble",
    )(blocks_at, near, far)


CORE, X, Y, Z_LOW, Z_HIGH = 1, 2, 4, 8, 16


def relative_places():
    places = np.zeros((32, 32), np.int32)
    for i in range(32):
        for b in range(32):
            bits = i ^ b
            x, y = int(bits & X > 0), int(bits & Y > 0)
            first, second = (y, x) if b & CORE else (x, y)
            low, high = int(bits & Z_LOW > 0), int(bits & Z_HIGH > 0)
            places[i, b] = 16 * (bits & CORE) + 8 * first + 4 * second + 2 * low + high
    return places


def exchange(values, even, odd):
    return lax.ppermute(
        values, "dp", [(i, i ^ (odd if i & CORE else even)) for i in range(32)]
    )


def added(a, b):
    return (a.astype(f32) + b.astype(f32)).astype(bf16)


def after(values, *earlier):
    return lax.optimization_barrier((values, *earlier))[0]


GATHER_HOPS = ((Z_HIGH, Z_HIGH), (Z_LOW, Z_LOW), (Y, X), (X, Y), (CORE, CORE))


def gather_blocks(*own):
    held = [part[None] for part in own]
    earlier = yield
    for hop in GATHER_HOPS:
        if earlier is not None:
            held[0] = after(held[0], *earlier)
        near, got = held[0], [exchange(part, *hop) for part in held]
        if hop[0] != CORE:
            held = [jnp.concatenate([jnp.concatenate(held, axis=2), jnp.concatenate(got, axis=2)], axis=0)]
        earlier = yield got[0], near


def fold(pairs):
    half = pairs[0][0].shape[0] // 2

    def joined(rows):
        return jnp.concatenate([added(kept[rows], got[rows]) for kept, got in pairs], axis=1)

    return joined(slice(half, 2 * half)), joined(slice(0, half))


def meet(parts):
    return [(near, exchange(far, CORE, CORE)) for near, far in parts]


def hop(state, even, odd):
    send, keep = state
    return keep, exchange(send, even, odd)


def total(pair):
    return pair[0][0].astype(f32) + pair[1][0].astype(f32)


def body(
    tokens, cotangent, lengths, w_qkv, w_out, w_up, w_down, bias_q, bias_v, bias_out,
    gain_one, shift_one, bias_up, bias_down, gain_two, shift_two,
):
    count = lax.axis_size("dp")
    index = lax.axis_index("dp")
    width = tokens.shape[1]
    units = w_up.shape[1]
    shard = w_qkv.shape[0]
    ratio = units // width
    small = jnp.concatenate(
        [bias_q, bias_v, bias_out, gain_one, shift_one, bias_down, gain_two, shift_two]
    )
    small = jnp.concatenate([small.reshape(8, shard).T, bias_up.reshape(shard, ratio)], axis=1)
    small = jnp.pad(small, ((0, 0), (0, 128 - small.shape[1])))
    up_out_shard = jnp.concatenate([w_up, w_out], axis=1)
    if count == BLOCKS:
        table = relative_places()
        core = np.arange(BLOCKS)[:, None] & CORE
        place = jnp.asarray(np.concatenate([table, core], axis=1).astype(np.int32))[index]
        blocks_at = jnp.asarray(np.argsort(table, axis=1).astype(np.int32))[index]
        first, second = gather_blocks(w_qkv, small), gather_blocks(up_out_shard)
        next(first)
        next(second)
        full_down = lax.all_gather(w_down, "dp", axis=0, tiled=True)
        hops = [first.send(None) for _ in range(4)]
        behind = [second.send([hops[1][0]])[0]]
        far, near = first.send([behind[0]])
        full_qkv = assemble(blocks_at, near, far).reshape(width, -1)
        behind.append(second.send([far])[0])
    else:
        place = jnp.arange(BLOCKS, dtype=jnp.int32) // 2
        place = jnp.append(place, 0)
        full_qkv, full_up_out, full_down = (
            lax.all_gather(part, "dp", axis=0, tiled=True)
            for part in (jnp.concatenate([w_qkv, small], axis=1), up_out_shard, w_down)
        )
    vectors = full_qkv[:, 3 * width :]
    full_bias_up = vectors[:, 8 : 8 + ratio].reshape(1, units)

    forward = []
    for g in range(width // COLS):
        held = tokens
        if count == BLOCKS and g:
            held = after(tokens, behind[g], forward[-1][3], *[full_down][: g - 1])
        forward.append(attend_forward(g, lengths, held, full_qkv))
        if count == BLOCKS and g < 2:
            behind.append(second.send([forward[-1][3], *[full_down][:g]])[0])
    if count == BLOCKS:
        far, near = second.send([forward[-1][3]])
        full_up_out = assemble(blocks_at, near, far).reshape(width, -1)
    (
        output, grad_one, grad_attn, grad_mixed, hidden_low, grad_branch, mixed, active, grad_up,
        gvec, gbu,
    ) = feed_forward(
        lengths, tokens, [part[3] for part in forward], cotangent, full_up_out, full_down,
        full_qkv, full_bias_up,
    )
    part_down = weight_grad_tall(place, active, grad_branch)
    part_up = weight_grad_wide(place, after(hidden_low, part_down[0]), grad_up, width)
    held = after(mixed, part_up[0])
    if count == BLOCKS:
        down = fold(meet([part_down]))
        held = after(held, down[0])
    part_out = weight_grad_wide(place, held, grad_attn, COLS)
    milestones = []

    def backward(g):
        held = after(grad_mixed, *milestones)
        query, keys, values, own_mixed, lse = forward[g]
        return attend_backward(g, lengths, place, tokens, query, keys, values, held, own_mixed, lse)

    if count != BLOCKS:
        groups = [backward(g) for g in range(width // COLS)]
        grad_tokens = token_grad(
            grad_one, [group[s] for s in range(3) for group in groups], full_qkv
        )
        gbias = jnp.concatenate([group[5] for group in groups], axis=1)
        def scattered(part):
            return lax.psum_scatter(part, "dp", scatter_dimension=0, tiled=True).astype(f32)

        def lined(halves):
            part = jnp.stack(halves, axis=1).reshape(BLOCKS, *halves[0].shape[1:])
            return part.transpose(0, 2, 1, 3).reshape(width, -1)

        part_qkv = [jnp.concatenate([group[h] for group in groups], axis=3) for h in (3, 4)]
        tall_down = jnp.stack(part_down, axis=1).reshape(units, width)
        return (
            output, grad_tokens, scattered(lined(part_qkv)), scattered(lined(part_out)),
            scattered(lined(part_up)), scattered(tall_down),
            scattered(gbias[0]), scattered(gbias[1]), scattered(gvec[5]), scattered(gvec[3]),
            scattered(gvec[4]), scattered(gbu[0]), scattered(gvec[2]), scattered(gvec[0]),
            scattered(gvec[1]),
        )

    def small_part(*all_lines):
        rows = []
        for lines in all_lines:
            line = jnp.concatenate(
                [
                    part.reshape(part.shape[0], BLOCKS, -1).transpose(1, 0, 2).reshape(BLOCKS, -1)
                    for part in lines
                ],
                axis=1,
            )
            rows.append(jnp.pad(line.astype(bf16), ((0, 0), (0, COLS - line.shape[1])))[:, None])
        rows = jnp.concatenate(rows, axis=1)[blocks_at]
        rows = jnp.pad(rows, ((0, 0), (0, 8 - rows.shape[1]), (0, 0)))
        return rows[: BLOCKS // 2], rows[BLOCKS // 2 :]

    def rows_of(halves):
        return [half.reshape(half.shape[0], -1, half.shape[-1]) for half in halves]

    down_first = hop(down, X, Y)
    up_met = meet([rows_of(part_up)])
    out_met = meet([rows_of(part_out)])
    up = fold(up_met)
    milestones += [part_out[0], up[0]]
    groups = [backward(0)]
    up_first = hop(up, X, Y)
    milestones[:] = [groups[0][0]]
    mlp = fold([down_first, up_first])
    milestones += [mlp[0]]
    groups.append(backward(1))
    mlp = fold([hop(mlp, Y, X)])
    early = fold(out_met + meet([rows_of(groups[0][3:5])]))
    milestones[:] = [groups[1][0], mlp[0], early[0]]
    groups.append(backward(2))
    mlp = fold([hop(mlp, Z_LOW, Z_LOW)])
    early_first = hop(early, X, Y)
    gbias = jnp.concatenate([group[5] for group in groups], axis=1)
    small_attn = small_part([gvec[:6], gbu], [gbias[:2]])
    late = fold(meet([rows_of(groups[1][3:5]), rows_of(groups[2][3:5]), small_attn]))
    late_first = hop((after(late[0], mlp[0]), late[1]), X, Y)
    grad_tokens = token_grad(
        grad_one, [group[s] for s in range(3) for group in groups], full_qkv
    )
    mlp = total(hop(mlp, Z_HIGH, Z_HIGH))
    attn = fold([early_first, late_first])
    attn = after(attn[0], mlp), attn[1]
    attn = fold([hop(attn, Y, X)])
    attn = fold([hop(attn, Z_LOW, Z_LOW)])
    attn = total(hop(attn, Z_HIGH, Z_HIGH))

    def wide_of(rows):
        return rows.reshape(-1, shard, width).transpose(1, 0, 2).reshape(shard, -1)

    tall = ratio * shard
    attn = [attn[i * shard : i * shard + shard] for i in range(12)] + [
        attn[12 * shard],
        attn[12 * shard + 1],
    ]
    line, line_attn = attn[12:]
    grad_out_weight = jnp.concatenate(attn[:3], axis=1)
    grad_qkv = jnp.concatenate([attn[3 + 3 * g + s] for s in range(3) for g in range(3)], axis=1)

    def piece(line, i):
        return line[i * shard : i * shard + shard]

    return (
        output, grad_tokens, grad_qkv, grad_out_weight,
        wide_of(mlp[tall:]), mlp[:tall],
        piece(line_attn, 0), piece(line_attn, 1), piece(line, 5), piece(line, 3), piece(line, 4),
        line[6 * shard : 6 * shard + tall], piece(line, 2), piece(line, 0), piece(line, 1),
    )


def solution(mesh):
    rows, vector = P("dp", None), P("dp")
    return jax.shard_map(
        body, mesh=mesh, in_specs=(rows,) * 7 + (vector,) * 9, out_specs=(rows,) * 6 + (vector,) * 9,
        check_vma=False,
    )
```

```python
import functools
import math

import jax
import jax.numpy as jnp
import numpy as np
from jax import lax
from jax.experimental import pallas as pl
from jax.experimental.pallas import tpu as pltpu
from jax.sharding import PartitionSpec as P

HD = 64
FORWARD_TILE = 512
BACKWARD_TILE = 256
FAR = 2.0**30
BITS = 11
COLS = 256
TB = 256
FB = 768
BLOCKS = 32
NORM_EPS = 1e-06
SCALE = 1.0 / math.sqrt(HD)
NT = (((1,), (1,)), ((), ()))
TN = (((0,), (0,)), ((), ()))
f32 = jnp.float32
bf16 = jnp.bfloat16


def dot(a, b, dims=(((1,), (0,)), ((), ()))):
    return lax.dot_general(a, b, dims, preferred_element_type=f32)


def ends_of(len_ref):
    ends, total = [], jnp.int32(0)
    for j in range(len_ref.shape[1]):
        total = total + len_ref[0, j]
        ends.append(total)
    return ends


def segment_of(position, ends):
    member = jnp.zeros_like(position)
    for end in ends:
        member = member + (position >= end).astype(jnp.int32)
    return jnp.where(position < ends[-1], member, position + len(ends))


def key_range(ends, first, last, tile):
    low, high = jnp.int32(0), jnp.int32(0)
    start = jnp.int32(0)
    for end in ends:
        low = jnp.where((first >= start) & (first < end), start, low)
        high = jnp.where((last >= start) & (last < end), end, high)
        start = end
    total = ends[-1]
    low = jnp.where(first >= total, first, low)
    high = jnp.where(last >= total, last + 1, high)
    return low // tile, (high + tile - 1) // tile


def other_half(own, other, h):
    return jnp.concatenate([other, own] if h % 2 else [own, other], axis=0)


def segment_codes(rows, ends):
    spot = lax.broadcasted_iota(jnp.int32, (HD, rows), 0)
    seg = segment_of(lax.broadcasted_iota(jnp.int32, (1, rows), 1), ends)
    bit = (seg >> (spot // 2)) & 1
    code_q = jnp.where(spot < 2 * BITS, jnp.where(spot % 2 == 0, bit, 1 - bit), 0)
    spot = lax.broadcasted_iota(jnp.int32, (rows, 128), 1) % HD
    seg = segment_of(lax.broadcasted_iota(jnp.int32, (rows, 128), 0), ends)
    bit = (seg >> (spot // 2)) & 1
    code_k = jnp.where(spot < 2 * BITS, jnp.where(spot % 2 == 0, 1 - bit, bit), 0)
    return code_q.astype(f32).astype(bf16), code_k.astype(f32) * -FAR


def pieces(value):
    high = value.astype(bf16)
    rest = value - high.astype(f32)
    middle = rest.astype(bf16)
    return [high, middle, (rest - middle.astype(f32)).astype(bf16)]


def attend_forward_kernel(
    group, len_ref, x_ref, wq_ref, wk_ref, wv_ref, vec_ref,
    q_ref, k_ref, v_ref, mixed_ref, lse_ref,
    qt_ref, ka_ref, vt_ref, code_q_ref, code_k_ref, acc_ref, top_ref, bias_ref,
):
    ends = ends_of(len_ref)

    code_q_ref[...], code_k = segment_codes(q_ref.shape[0], ends)
    code_k_ref[...] = code_k.astype(bf16)
    bias_ref[...] = vec_ref[...].astype(f32).T[:8]

    rows, cols = q_ref.shape
    heads = cols // HD
    own_cols = slice(group * cols, group * cols + cols)
    x = x_ref[...]
    query = (dot(x, wq_ref[...]) + bias_ref[0:1, own_cols]).astype(bf16)
    q_ref[...] = query
    keys = dot(x, wk_ref[...]).astype(bf16)
    k_ref[...] = keys
    value = (dot(x, wv_ref[...]) + bias_ref[1:2, own_cols]).astype(bf16)
    v_ref[...] = value
    turned, turned_value = (query * bf16(SCALE)).T, value.T
    lane = lax.broadcasted_iota(jnp.int32, (rows, 128), 1)
    for h in range(heads):
        part = slice(h * HD, h * HD + HD)
        own = (lane >= HD) if h % 2 else (lane < HD)
        qt_ref[h] = other_half(turned[part], code_q_ref[...], h)
        ka_ref[h] = jnp.where(own, keys[:, 128 * (h // 2) : 128 * (h // 2) + 128], code_k_ref[...])
        vt_ref[h, :HD] = turned_value[part]
        vt_ref[h, HD:] = jnp.ones((16, rows), bf16)

    def q_step(qi, _):
        q_cols = pl.ds(pl.multiple_of(qi * FORWARD_TILE, FORWARD_TILE), FORWARD_TILE)
        low, high = key_range(ends, qi * FORWARD_TILE, qi * FORWARD_TILE + FORWARD_TILE - 1, FORWARD_TILE)
        acc_ref[...] = jnp.zeros_like(acc_ref)
        top_ref[...] = jnp.full_like(top_ref, -3e38)

        def k_step(ki, _):
            k_rows = pl.ds(pl.multiple_of(ki * FORWARD_TILE, FORWARD_TILE), FORWARD_TILE)
            tops = top_ref[...]
            new_tops = []

            def scores_of(h):
                return dot(ka_ref[h, k_rows, :], qt_ref[h, :, q_cols])

            ahead = [scores_of(h) for h in range(1)]
            pending = []

            def finish(h, low_weights, fade):
                acc_ref[h] = acc_ref[h] * fade + dot(vt_ref[h, :, k_rows], low_weights)

            for h in range(heads):
                if h + 1 < heads:
                    ahead.append(scores_of(h + 1))
                scores = ahead[h]
                ahead[h] = None
                before = tops[h : h + 1]
                top = jnp.maximum(before, jnp.max(scores, axis=0, keepdims=True))
                new_tops.append(top)
                pending.append((h, jnp.exp(scores - top).astype(bf16), jnp.exp(before - top)))
                if len(pending) > 0:
                    finish(*pending.pop(0))
            for item in pending:
                finish(*item)
            spare = [jnp.zeros((8 - heads, FORWARD_TILE), f32)]
            top_ref[...] = jnp.concatenate(new_tops + spare, axis=0)
            return 0

        lax.fori_loop(low, high, k_step, 0)
        totals = jnp.concatenate([acc_ref[h, HD : HD + 1] for h in range(heads)], axis=0)
        for p in range(heads // 2):
            halves = [acc_ref[h, :HD] / totals[h : h + 1] for h in (2 * p, 2 * p + 1)]
            mixed = jnp.concatenate(halves, axis=0)
            mixed_ref[q_cols, 128 * p : 128 * p + 128] = mixed.T.astype(bf16)
        lse = top_ref[0:heads] + jnp.log(totals)
        lse_ref[0, :, q_cols] = jnp.concatenate([lse, jnp.zeros((8 - heads, FORWARD_TILE), f32)], axis=0)
        return 0

    lax.fori_loop(0, rows // FORWARD_TILE, q_step, 0)


def attend_forward(group, lengths, tokens, full_qkv):
    rows, width = tokens.shape
    cols = COLS
    groups = width // cols
    heads = cols // HD
    low = jax.ShapeDtypeStruct((rows, cols), bf16)
    own = pl.BlockSpec((rows, cols), lambda g: (0, 0))
    return pl.pallas_call(
        functools.partial(attend_forward_kernel, group),
        grid=(1,),
        in_specs=[
            pl.BlockSpec(memory_space=pltpu.SMEM),
            pl.BlockSpec((rows, width), lambda g: (0, 0)),
            pl.BlockSpec((width, cols), lambda g: (0, group)),
            pl.BlockSpec((width, cols), lambda g: (0, group + groups)),
            pl.BlockSpec((width, cols), lambda g: (0, group + 2 * groups)),
            pl.BlockSpec((width, 128), lambda g: (0, 3 * width // 128)),
        ],
        out_specs=[own] * 4 + [pl.BlockSpec((1, 8, rows), lambda g: (0, 0, 0))],
        out_shape=[low] * 4 + [jax.ShapeDtypeStruct((1, 8, rows), f32)],
        scratch_shapes=[
            pltpu.VMEM((heads, 128, rows), bf16),
            pltpu.VMEM((heads, rows, 128), bf16),
            pltpu.VMEM((heads, HD + 16, rows), bf16),
            pltpu.VMEM((HD, rows), bf16),
            pltpu.VMEM((rows, 128), bf16),
            pltpu.VMEM((heads, HD + 16, FORWARD_TILE), f32),
            pltpu.VMEM((8, FORWARD_TILE), f32),
            pltpu.VMEM((8, width), f32),
        ],
        compiler_params=pltpu.CompilerParams(vmem_limit_bytes=60 << 20),
        cost_estimate=pl.CostEstimate(flops=12 * rows * width * width, bytes_accessed=12 << 20, transcendentals=0),
        name="attend_forward",
    )(lengths, tokens, full_qkv, full_qkv, full_qkv, full_qkv)


def feed_forward_kernel(
    len_ref, x_ref, mixed_a_ref, mixed_b_ref, mixed_c_ref, cot_ref, wo_ref, wu_ref, wd_ref, vec_ref, bu_ref,
    out_ref, gp_ref, ga_ref, gm_ref, hl_ref, gb_ref, mixed_ref, act_ref, gu_ref, gvec_ref, gbu_ref,
    slope_ref, rows_ref,
):
    step = pl.program_id(0)
    rows, width = x_ref.shape
    hidden_units = bu_ref.shape[1]

    @pl.when(step == 0)
    def _():
        gvec_ref[...] = jnp.zeros_like(gvec_ref)
        gbu_ref[...] = jnp.zeros_like(gbu_ref)
        rows_ref[...] = vec_ref[...].astype(f32).T[:8]

    total = ends_of(len_ref)[-1]
    position = step * rows + lax.broadcasted_iota(jnp.int32, (rows, 1), 0)
    valid = (position < total).astype(f32)

    def vec(i):
        return rows_ref[i + 2 : i + 3, :]

    def norm(values):
        centered = values - jnp.mean(values, axis=1, keepdims=True)
        scale = lax.rsqrt(jnp.mean(centered * centered, axis=1, keepdims=True) + NORM_EPS)
        return centered * scale, scale

    def norm_back(grad, gain, unit, scale):
        grad = grad * gain
        mean_grad = jnp.mean(grad, axis=1, keepdims=True)
        mean_unit = jnp.mean(grad * unit, axis=1, keepdims=True)
        return scale * (grad - mean_grad - unit * mean_unit)

    def add_vec(i, value):
        gvec_ref[i : i + 1, :] += jnp.sum(value, axis=0, keepdims=True)

    mixed_ref[...] = jnp.concatenate(
        [mixed_a_ref[...], mixed_b_ref[...], mixed_c_ref[...]], axis=1
    )
    pre_one = x_ref[...].astype(f32) + dot(mixed_ref[...], wo_ref[...]) + vec(0)
    unit_one, scale_one = norm(pre_one)
    hidden = unit_one * vec(1) + vec(2)
    hidden_low = hidden.astype(bf16)
    hl_ref[...] = hidden_low
    branch = jnp.zeros((rows, width), f32)
    parts = [slice(f * FB, f * FB + FB) for f in range(hidden_units // FB)]
    ahead = dot(hidden_low, wu_ref[:, parts[0]])
    for f, part in enumerate(parts):
        up = ahead + bu_ref[:, part].astype(f32)
        if f + 1 < len(parts):
            ahead = dot(hidden_low, wu_ref[:, parts[f + 1]])
        bell = jnp.exp(up * up * -0.5)
        t = 1.0 / (1.0 + (0.3275911 * math.sqrt(0.5)) * jnp.abs(up))
        poly = 0.5 * 1.061405429 * t - 0.5 * 1.453152027
        poly = poly * t + 0.5 * 1.421413741
        poly = poly * t - 0.5 * 0.284496736
        poly = poly * t + 0.5 * 0.254829592
        tail = poly * t * bell
        share = jnp.where(up >= 0, 1.0 - tail, tail)
        active = (up * share).astype(bf16)
        act_ref[:, part] = active
        slope_ref[:, part] = share + up * bell * (1.0 / math.sqrt(2.0 * math.pi))
        branch = branch + dot(active, wd_ref[part, :])
    unit_two, scale_two = norm(hidden + branch + vec(3))
    out_ref[...] = (valid * (unit_two * vec(4) + vec(5))).astype(bf16)
    grad_out = valid * cot_ref[...].astype(f32)
    add_vec(0, grad_out * unit_two)
    add_vec(1, grad_out)
    grad_two = norm_back(grad_out, vec(4), unit_two, scale_two)
    grad_branch = grad_two.astype(bf16)
    gb_ref[...] = grad_branch
    add_vec(2, grad_branch.astype(f32))
    grad_hidden = grad_two
    ahead = dot(grad_branch, wd_ref[parts[0], :], NT)
    for f, part in enumerate(parts):
        grad_up = (ahead * slope_ref[:, part]).astype(bf16)
        if f + 1 < len(parts):
            ahead = dot(grad_branch, wd_ref[parts[f + 1], :], NT)
        gu_ref[:, part] = grad_up
        gbu_ref[:, part] += jnp.sum(grad_up.astype(f32), axis=0, keepdims=True)
        grad_hidden = grad_hidden + dot(grad_up, wu_ref[:, part], NT)
    add_vec(3, grad_hidden * unit_one)
    add_vec(4, grad_hidden)
    grad_one = norm_back(grad_hidden, vec(1), unit_one, scale_one)
    gp_ref[...] = grad_one
    grad_attn = grad_one.astype(bf16)
    ga_ref[...] = grad_attn
    add_vec(5, grad_attn.astype(f32))
    gm_ref[...] = dot(grad_attn, wo_ref[...], NT).astype(bf16)


def feed_forward(lengths, tokens, mixed, cotangent, full_up_out, full_down, full_qkv, bias_up):
    rows, width = tokens.shape
    units = bias_up.shape[1]
    by_rows = pl.BlockSpec((TB, width), lambda i: (i, 0))
    by_units = pl.BlockSpec((TB, units), lambda i: (i, 0))

    def whole(shape, column=0):
        return pl.BlockSpec(shape, lambda i: (0, column), pipeline_mode=pl.Buffered(1))

    def kept(shape):
        return pl.BlockSpec(shape, lambda i: (0,) * len(shape))

    low = jax.ShapeDtypeStruct((rows, width), bf16)
    wide = jax.ShapeDtypeStruct((rows, units), bf16)
    return pl.pallas_call(
        feed_forward_kernel,
        grid=(rows // TB,),
        in_specs=[
            pl.BlockSpec(memory_space=pltpu.SMEM),
            by_rows, *[pl.BlockSpec((TB, part.shape[1]), lambda i: (i, 0)) for part in mixed], by_rows,
            whole((width, width), units // width), whole((width, units)), whole(full_down.shape),
            whole((width, 128), 3 * width // 128), whole(bias_up.shape),
        ],
        out_specs=[by_rows] * 7 + [by_units] * 2 + [kept((8, width)), kept((1, units))],
        out_shape=[low, jax.ShapeDtypeStruct((rows, width), f32), low, low, low, low, low, wide, wide,
                   jax.ShapeDtypeStruct((8, width), f32), jax.ShapeDtypeStruct((1, units), f32)],
        scratch_shapes=[pltpu.VMEM((TB, units), f32), pltpu.VMEM((8, width), f32)],
        compiler_params=pltpu.CompilerParams(vmem_limit_bytes=56 << 20),
        cost_estimate=pl.CostEstimate(flops=8 * rows * width * units + 4 * rows * width * width, bytes_accessed=40 << 20, transcendentals=0),
        name="feed_forward",
    )(lengths, tokens, *mixed, cotangent, full_up_out, full_up_out, full_down, full_qkv, bias_up)


def store_blocks(place_ref, total_ref, near_ref, far_ref, at, base=0):
    size = near_ref.shape[-2]
    own = place_ref[BLOCKS]
    for pair in range(total_ref.shape[0] // (2 * size)):
        for ref, core in ((near_ref, own), (far_ref, 1 - own)):
            block = 2 * pair + core
            rows = pl.ds(pl.multiple_of(block * size, size), size)
            ref[(place_ref[base + block] % (BLOCKS // 2), *at)] = total_ref[rows, :].astype(bf16)


def weight_grad_kernel(place_ref, left_ref, right_ref, near_ref, far_ref, left_t_ref, total_ref):
    @pl.when(pl.program_id(0) == 0)
    def _():
        left_t_ref[...] = left_ref[...].T

    total_ref[...] = dot(left_t_ref[...], right_ref[...])
    store_blocks(place_ref, total_ref, near_ref, far_ref, (0,))


def weight_grad_wide(place, left, right, cols):
    rows, width = left.shape
    groups = right.shape[1] // cols
    size = width // BLOCKS
    return pl.pallas_call(
        weight_grad_kernel,
        grid=(groups,),
        in_specs=[
            pl.BlockSpec(memory_space=pltpu.SMEM),
            pl.BlockSpec((rows, width), lambda g: (0, 0)),
            pl.BlockSpec((rows, cols), lambda g: (0, g)),
        ],
        out_specs=[pl.BlockSpec((BLOCKS // 2, 1, size, cols), lambda g: (0, g, 0, 0))] * 2,
        out_shape=[jax.ShapeDtypeStruct((BLOCKS // 2, groups, size, cols), bf16)] * 2,
        scratch_shapes=[pltpu.VMEM((width, rows), bf16), pltpu.VMEM((width, cols), f32)],
        compiler_params=pltpu.CompilerParams(vmem_limit_bytes=20 << 20),
        cost_estimate=pl.CostEstimate(flops=2 * rows * width * right.shape[1], bytes_accessed=12 << 20, transcendentals=0),
        name="weight_grad_wide",
    )(place, left, right)


def weight_grad_tall_kernel(place_ref, left_ref, right_ref, near_ref, far_ref, total_ref):
    total_ref[...] = dot(left_ref[...], right_ref[...], TN)
    base = pl.program_id(0) * (total_ref.shape[0] // near_ref.shape[1])
    store_blocks(place_ref, total_ref, near_ref, far_ref, (), base)


def weight_grad_tall(place, left, right):
    rows, units = left.shape
    width = right.shape[1]
    size = units // BLOCKS
    return pl.pallas_call(
        weight_grad_tall_kernel,
        grid=(units // width,),
        in_specs=[
            pl.BlockSpec(memory_space=pltpu.SMEM),
            pl.BlockSpec((rows, width), lambda g: (0, g)),
            pl.BlockSpec((rows, width), lambda g: (0, 0)),
        ],
        out_specs=[pl.BlockSpec((BLOCKS // 2, size, width), lambda g: (0, 0, 0))] * 2,
        out_shape=[jax.ShapeDtypeStruct((BLOCKS // 2, size, width), bf16)] * 2,
        scratch_shapes=[pltpu.VMEM((width, width), f32)],
        compiler_params=pltpu.CompilerParams(vmem_limit_bytes=20 << 20),
        cost_estimate=pl.CostEstimate(flops=2 * rows * width * units, bytes_accessed=12 << 20, transcendentals=0),
        name="weight_grad_tall",
    )(place, left, right)


def attend_backward_kernel(
    len_ref, place_ref, xt_ref, q_ref, k_ref, v_ref, do_ref, o_ref, lse_ref,
    dq_ref, dk_ref, dv_ref, near_ref, far_ref, gbias_ref,
    qs_ref, dos_ref, qt_ref, dot_ref, ka_ref, va_ref, kt_ref, code_q_ref, code_k_ref,
    dqt_ref, dk_acc, dv_acc, total_ref,
):
    rows, cols = q_ref.shape
    heads = cols // HD
    ends = ends_of(len_ref)

    code_q, code_k = segment_codes(rows, ends)
    code_q_ref[...] = code_q
    spot = lax.broadcasted_iota(jnp.int32, (rows, 128), 1) % HD
    code_k_ref[...] = jnp.where((spot >= 2 * BITS) & (spot < 2 * BITS + 3), 1.0, code_k).astype(bf16)

    query, keys, values, grad = q_ref[...], k_ref[...], v_ref[...], do_ref[...]
    lane = lax.broadcasted_iota(jnp.int32, (rows, 128), 1)
    for h in range(heads):
        pair = slice(128 * (h // 2), 128 * (h // 2) + 128)
        own = (lane >= HD) if h % 2 else (lane < HD)
        qs_ref[h] = jnp.where(own, query[:, pair] * bf16(SCALE), bf16(0))
        dos_ref[h] = jnp.where(own, grad[:, pair], bf16(0))
    kt_ref[...] = keys.T
    product = grad.astype(f32) * o_ref[...].astype(f32)
    high_part = product.astype(bf16)
    low_part = (product - high_part.astype(f32)).astype(bf16)
    pick = (
        lax.broadcasted_iota(jnp.int32, (8, cols), 1) // HD
        == lax.broadcasted_iota(jnp.int32, (8, cols), 0)
    ).astype(bf16)
    delta = dot(pick, high_part, NT) + dot(pick, low_part, NT)
    turned, turned_grad = (query * bf16(SCALE)).T, grad.T
    lane = lax.broadcasted_iota(jnp.int32, (rows, 128), 1)
    ones = jnp.where(lane % HD < 3, 1.0, 0.0).astype(bf16)
    for h in range(heads):
        part = slice(h * HD, h * HD + HD)
        pair = slice(128 * (h // 2), 128 * (h // 2) + 128)
        own = (lane >= HD) if h % 2 else (lane < HD)
        code = jnp.concatenate(
            [code_q_ref[: 2 * BITS].astype(f32)]
            + [piece.astype(f32) for piece in pieces(-lse_ref[0, h : h + 1, :])]
            + [jnp.zeros((HD - 2 * BITS - 3, rows), f32)],
            axis=0,
        ).astype(bf16)
        qt_ref[h] = other_half(turned[part], code, h)
        ka_ref[h] = jnp.where(own, keys[:, pair], code_k_ref[...])
        shift = jnp.concatenate(
            [piece.astype(f32) for piece in pieces(-delta[h : h + 1, :])]
            + [jnp.zeros((HD - 3, rows), f32)],
            axis=0,
        ).astype(bf16)
        dot_ref[h] = other_half(turned_grad[part], shift, h)
        va_ref[h] = jnp.where(own, values[:, pair], ones)
    dk_acc[...] = jnp.zeros_like(dk_acc)
    dv_acc[...] = jnp.zeros_like(dv_acc)

    def q_step(qi, _):
        q_rows = pl.ds(pl.multiple_of(qi * BACKWARD_TILE, BACKWARD_TILE), BACKWARD_TILE)
        low, high = key_range(ends, qi * BACKWARD_TILE, qi * BACKWARD_TILE + BACKWARD_TILE - 1, BACKWARD_TILE)
        dqt_ref[...] = jnp.zeros_like(dqt_ref)

        def k_step(ki, _):
            k_rows = pl.ds(pl.multiple_of(ki * BACKWARD_TILE, BACKWARD_TILE), BACKWARD_TILE)

            def products_of(h):
                return (
                    dot(ka_ref[h, k_rows, :], qt_ref[h, :, q_rows]),
                    dot(va_ref[h, k_rows, :], dot_ref[h, :, q_rows]),
                )

            ahead = [products_of(h) for h in range(2)]
            pending = []

            def finish(p, probs_a, grads_a, probs_b, grads_b):
                pair = slice(128 * p, 128 * p + 128)
                dv_acc[k_rows, pair] += dot(probs_a, dos_ref[2 * p, q_rows, :]) + dot(
                    probs_b, dos_ref[2 * p + 1, q_rows, :]
                )
                dk_acc[k_rows, pair] += dot(grads_a, qs_ref[2 * p, q_rows, :]) + dot(
                    grads_b, qs_ref[2 * p + 1, q_rows, :]
                )
                for h, grads in ((2 * p, grads_a), (2 * p + 1, grads_b)):
                    part = slice(h * HD, h * HD + HD)
                    dqt_ref[part, :] += dot(kt_ref[part, k_rows], grads)

            held = []
            for h in range(heads):
                if h + 2 < heads:
                    ahead.append(products_of(h + 2))
                scores, grad_probs = ahead[h]
                ahead[h] = None
                probs = jnp.exp(scores)
                grad_scores = (probs * grad_probs).astype(bf16)
                held += [probs.astype(bf16), grad_scores]
                if h % 2:
                    pending.append((h // 2, *held))
                    held = []
                if h % 2 and len(pending) > 1:
                    finish(*pending.pop(0))
            for item in pending:
                finish(*item)
            return 0

        lax.fori_loop(low, high, k_step, 0)
        dq_ref[q_rows, :] = (dqt_ref[...] * SCALE).T.astype(bf16)
        return 0

    lax.fori_loop(0, rows // BACKWARD_TILE, q_step, 0)
    dk_ref[...] = dk_acc[...].astype(bf16)
    dv_ref[...] = dv_acc[...].astype(bf16)
    for s, part in enumerate((dq_ref, dk_ref, dv_ref)):
        total_ref[...] = dot(xt_ref[...], part[...])
        store_blocks(place_ref, total_ref, near_ref, far_ref, (s,))
    gbias_ref[0:1, :] = jnp.sum(dq_ref[...].astype(f32), axis=0, keepdims=True)
    gbias_ref[1:2, :] = jnp.sum(dv_ref[...].astype(f32), axis=0, keepdims=True)


def attend_backward(group, lengths, place, turned, query, keys, values, grad_mixed, mixed, lse):
    width, rows = turned.shape
    cols = COLS
    heads = cols // HD
    size = width // BLOCKS
    by_group = pl.BlockSpec((rows, cols), lambda g: (0, group))
    own = pl.BlockSpec((rows, cols), lambda g: (0, 0))
    low = jax.ShapeDtypeStruct((rows, cols), bf16)
    return pl.pallas_call(
        attend_backward_kernel,
        grid=(1,),
        in_specs=[
            pl.BlockSpec(memory_space=pltpu.SMEM),
            pl.BlockSpec(memory_space=pltpu.SMEM),
            pl.BlockSpec((width, rows), lambda g: (0, 0)),
        ]
        + [own] * 3
        + [by_group]
        + [own]
        + [pl.BlockSpec((1, 8, rows), lambda g: (0, 0, 0))],
        out_specs=[own] * 3
        + [
            pl.BlockSpec((BLOCKS // 2, 3, size, cols), lambda g: (0, 0, 0, 0)),
            pl.BlockSpec((BLOCKS // 2, 3, size, cols), lambda g: (0, 0, 0, 0)),
            pl.BlockSpec((8, cols), lambda g: (0, 0)),
        ],
        out_shape=[low] * 3
        + [
            jax.ShapeDtypeStruct((BLOCKS // 2, 3, size, cols), bf16),
            jax.ShapeDtypeStruct((BLOCKS // 2, 3, size, cols), bf16),
            jax.ShapeDtypeStruct((8, cols), f32),
        ],
        scratch_shapes=[
            pltpu.VMEM((heads, rows, 128), bf16),
            pltpu.VMEM((heads, rows, 128), bf16),
            pltpu.VMEM((heads, 128, rows), bf16),
            pltpu.VMEM((heads, 128, rows), bf16),
            pltpu.VMEM((heads, rows, 128), bf16),
            pltpu.VMEM((heads, rows, 128), bf16),
            pltpu.VMEM((cols, rows), bf16),
            pltpu.VMEM((HD, rows), bf16),
            pltpu.VMEM((rows, 128), bf16),
            pltpu.VMEM((cols, BACKWARD_TILE), f32),
            pltpu.VMEM((rows, cols), f32),
            pltpu.VMEM((rows, cols), f32),
            pltpu.VMEM((width, cols), f32),
        ],
        compiler_params=pltpu.CompilerParams(vmem_limit_bytes=44 << 20),
        cost_estimate=pl.CostEstimate(flops=12 * rows * width * width, bytes_accessed=16 << 20, transcendentals=0),
        name="attend_backward",
    )(lengths, place, turned, query, keys, values, grad_mixed, mixed, lse)


def token_grad_kernel(gp_ref, *refs):
    *grads, w_ref, out_ref = refs
    total = gp_ref[...]
    cols = grads[0].shape[1]
    for i, grad in enumerate(grads):
        total = total + dot(grad[...], w_ref[:, i * cols : i * cols + cols], NT)
    out_ref[...] = total


def token_grad(grad_one, grads, full_qkv):
    rows, width = grad_one.shape
    cols = grads[0].shape[1]
    by_rows = pl.BlockSpec((TB, width), lambda i: (i, 0))
    return pl.pallas_call(
        token_grad_kernel,
        grid=(rows // TB,),
        in_specs=[by_rows]
        + [pl.BlockSpec((TB, cols), lambda i: (i, 0))] * len(grads)
        + [pl.BlockSpec((width, 3 * width), lambda i: (0, 0), pipeline_mode=pl.Buffered(1))],
        out_specs=by_rows,
        out_shape=jax.ShapeDtypeStruct((rows, width), f32),
        compiler_params=pltpu.CompilerParams(vmem_limit_bytes=28 << 20),
        cost_estimate=pl.CostEstimate(flops=6 * rows * width * width, bytes_accessed=14 << 20, transcendentals=0),
        name="token_grad",
    )(grad_one, *grads, full_qkv)


def assemble_kernel(blocks_ref, near_ref, far_ref, out_ref):
    count = near_ref.shape[0]
    for m in range(count):
        out_ref[blocks_ref[m]] = near_ref[m]
        out_ref[blocks_ref[count + m]] = far_ref[m]


def assemble(blocks_at, near, far):
    rows, cols = near.shape[1:]
    parts = 1
    while cols % (2 * parts * 128) == 0 and cols // parts > 1024:
        parts *= 2
    while cols // parts > 1024 and cols % (3 * parts * 128) == 0:
        parts *= 3
    by_cols = pl.BlockSpec((near.shape[0], rows, cols // parts), lambda i: (0, 0, i))
    return pl.pallas_call(
        assemble_kernel,
        grid=(parts,),
        in_specs=[pl.BlockSpec(memory_space=pltpu.SMEM), by_cols, by_cols],
        out_specs=pl.BlockSpec((BLOCKS, rows, cols // parts), lambda i: (0, 0, i)),
        out_shape=jax.ShapeDtypeStruct((BLOCKS, rows, cols), near.dtype),
        compiler_params=pltpu.CompilerParams(vmem_limit_bytes=20 << 20),
        cost_estimate=pl.CostEstimate(flops=0, bytes_accessed=4 * near.size * 2, transcendentals=0),
        name="assemble",
    )(blocks_at, near, far)


CORE, X, Y, Z_LOW, Z_HIGH = 1, 2, 4, 8, 16


def relative_places():
    places = np.zeros((32, 32), np.int32)
    for i in range(32):
        for b in range(32):
            bits = i ^ b
            x, y = int(bits & X > 0), int(bits & Y > 0)
            first, second = (y, x) if b & CORE else (x, y)
            low, high = int(bits & Z_LOW > 0), int(bits & Z_HIGH > 0)
            places[i, b] = 16 * (bits & CORE) + 8 * first + 4 * second + 2 * low + high
    return places


def exchange(values, even, odd):
    return lax.ppermute(
        values, "dp", [(i, i ^ (odd if i & CORE else even)) for i in range(32)]
    )


def added(a, b):
    return (a.astype(f32) + b.astype(f32)).astype(bf16)


def after(values, *earlier):
    return lax.optimization_barrier((values, *earlier))[0]


GATHER_HOPS = ((Z_HIGH, Z_HIGH), (Z_LOW, Z_LOW), (Y, X), (X, Y), (CORE, CORE))


def gather_blocks(*own):
    held = [part[None] for part in own]
    earlier = yield
    for hop in GATHER_HOPS:
        if earlier is not None:
            held[0] = after(held[0], *earlier)
        near, got = held[0], [exchange(part, *hop) for part in held]
        if hop[0] != CORE:
            held = [jnp.concatenate([jnp.concatenate(held, axis=2), jnp.concatenate(got, axis=2)], axis=0)]
        earlier = yield got[0], near


def fold(pairs):
    half = pairs[0][0].shape[0] // 2

    def joined(rows):
        return jnp.concatenate([added(kept[rows], got[rows]) for kept, got in pairs], axis=1)

    return joined(slice(half, 2 * half)), joined(slice(0, half))


def meet(parts):
    return [(near, exchange(far, CORE, CORE)) for near, far in parts]


def hop(state, even, odd):
    send, keep = state
    return keep, exchange(send, even, odd)


def total(pair):
    return pair[0][0].astype(f32) + pair[1][0].astype(f32)


def body(
    tokens, cotangent, lengths, w_qkv, w_out, w_up, w_down, bias_q, bias_v, bias_out,
    gain_one, shift_one, bias_up, bias_down, gain_two, shift_two,
):
    count = lax.axis_size("dp")
    index = lax.axis_index("dp")
    width = tokens.shape[1]
    units = w_up.shape[1]
    shard = w_qkv.shape[0]
    ratio = units // width
    small = jnp.concatenate(
        [bias_q, bias_v, bias_out, gain_one, shift_one, bias_down, gain_two, shift_two]
    )
    small = jnp.concatenate([small.reshape(8, shard).T, bias_up.reshape(shard, ratio)], axis=1)
    small = jnp.pad(small, ((0, 0), (0, 128 - small.shape[1])))
    up_out_shard = jnp.concatenate([w_up, w_out], axis=1)
    if count == BLOCKS:
        table = relative_places()
        core = np.arange(BLOCKS)[:, None] & CORE
        place = jnp.asarray(np.concatenate([table, core], axis=1).astype(np.int32))[index]
        blocks_at = jnp.asarray(np.argsort(table, axis=1).astype(np.int32))[index]
        first, second = gather_blocks(w_qkv, small), gather_blocks(up_out_shard)
        next(first)
        next(second)
        full_down = lax.all_gather(w_down, "dp", axis=0, tiled=True)
        hops = [first.send(None) for _ in range(4)]
        behind = [second.send([hops[1][0]])[0]]
        far, near = first.send([behind[0]])
        full_qkv = assemble(blocks_at, near, far).reshape(width, -1)
        behind.append(second.send([far])[0])
    else:
        place = jnp.arange(BLOCKS, dtype=jnp.int32) // 2
        place = jnp.append(place, 0)
        full_qkv, full_up_out, full_down = (
            lax.all_gather(part, "dp", axis=0, tiled=True)
            for part in (jnp.concatenate([w_qkv, small], axis=1), up_out_shard, w_down)
        )
    vectors = full_qkv[:, 3 * width :]
    full_bias_up = vectors[:, 8 : 8 + ratio].reshape(1, units)

    turned = tokens.T
    forward = []
    for g in range(width // COLS):
        held = after(tokens, turned)
        if count == BLOCKS and g:
            held = after(tokens, behind[g], forward[-1][3], *[full_down][: g - 1])
        forward.append(attend_forward(g, lengths, held, full_qkv))
        if count == BLOCKS and g < 2:
            behind.append(second.send([forward[-1][3], *[full_down][:g]])[0])
    if count == BLOCKS:
        far, near = second.send([forward[-1][3]])
        full_up_out = assemble(blocks_at, near, far).reshape(width, -1)
    (
        output, grad_one, grad_attn, grad_mixed, hidden_low, grad_branch, mixed, active, grad_up,
        gvec, gbu,
    ) = feed_forward(
        lengths, tokens, [part[3] for part in forward], cotangent, full_up_out, full_down,
        full_qkv, full_bias_up,
    )
    part_down = weight_grad_tall(place, active, grad_branch)
    part_up = weight_grad_wide(place, after(hidden_low, part_down[0]), grad_up, width)
    held = after(mixed, part_up[0])
    if count == BLOCKS:
        down = fold(meet([part_down]))
        held = after(held, down[0])
    part_out = weight_grad_wide(place, held, grad_attn, COLS)
    milestones = []

    def backward(g):
        held = after(grad_mixed, *milestones)
        query, keys, values, own_mixed, lse = forward[g]
        return attend_backward(g, lengths, place, turned, query, keys, values, held, own_mixed, lse)

    if count != BLOCKS:
        groups = [backward(g) for g in range(width // COLS)]
        grad_tokens = token_grad(
            grad_one, [group[s] for s in range(3) for group in groups], full_qkv
        )
        gbias = jnp.concatenate([group[5] for group in groups], axis=1)
        def scattered(part):
            return lax.psum_scatter(part, "dp", scatter_dimension=0, tiled=True).astype(f32)

        def lined(halves):
            part = jnp.stack(halves, axis=1).reshape(BLOCKS, *halves[0].shape[1:])
            return part.transpose(0, 2, 1, 3).reshape(width, -1)

        part_qkv = [jnp.concatenate([group[h] for group in groups], axis=3) for h in (3, 4)]
        tall_down = jnp.stack(part_down, axis=1).reshape(units, width)
        return (
            output, grad_tokens, scattered(lined(part_qkv)), scattered(lined(part_out)),
            scattered(lined(part_up)), scattered(tall_down),
            scattered(gbias[0]), scattered(gbias[1]), scattered(gvec[5]), scattered(gvec[3]),
            scattered(gvec[4]), scattered(gbu[0]), scattered(gvec[2]), scattered(gvec[0]),
            scattered(gvec[1]),
        )

    def small_part(*all_lines):
        rows = []
        for lines in all_lines:
            line = jnp.concatenate(
                [
                    part.reshape(part.shape[0], BLOCKS, -1).transpose(1, 0, 2).reshape(BLOCKS, -1)
                    for part in lines
                ],
                axis=1,
            )
            rows.append(jnp.pad(line.astype(bf16), ((0, 0), (0, COLS - line.shape[1])))[:, None])
        rows = jnp.concatenate(rows, axis=1)[blocks_at]
        rows = jnp.pad(rows, ((0, 0), (0, 8 - rows.shape[1]), (0, 0)))
        return rows[: BLOCKS // 2], rows[BLOCKS // 2 :]

    def rows_of(halves):
        return [half.reshape(half.shape[0], -1, half.shape[-1]) for half in halves]

    down_first = hop(down, X, Y)
    up_met = meet([rows_of(part_up)])
    out_met = meet([rows_of(part_out)])
    up = fold(up_met)
    milestones += [part_out[0], up[0]]
    groups = [backward(0)]
    up_first = hop(up, X, Y)
    milestones[:] = [groups[0][0]]
    mlp = fold([down_first, up_first])
    milestones += [mlp[0]]
    groups.append(backward(1))
    mlp = fold([hop(mlp, Y, X)])
    early = fold(out_met + meet([rows_of(groups[0][3:5])]))
    milestones[:] = [groups[1][0], mlp[0], early[0]]
    groups.append(backward(2))
    mlp = fold([hop(mlp, Z_LOW, Z_LOW)])
    early_first = hop(early, X, Y)
    gbias = jnp.concatenate([group[5] for group in groups], axis=1)
    small_attn = small_part([gvec[:6], gbu], [gbias[:2]])
    late = fold(meet([rows_of(groups[1][3:5]), rows_of(groups[2][3:5]), small_attn]))
    late_first = hop((after(late[0], mlp[0]), late[1]), X, Y)
    grad_tokens = token_grad(
        grad_one, [group[s] for s in range(3) for group in groups], full_qkv
    )
    mlp = total(hop(mlp, Z_HIGH, Z_HIGH))
    attn = fold([early_first, late_first])
    attn = after(attn[0], mlp), attn[1]
    attn = fold([hop(attn, Y, X)])
    attn = fold([hop(attn, Z_LOW, Z_LOW)])
    attn = total(hop(attn, Z_HIGH, Z_HIGH))

    def wide_of(rows):
        return rows.reshape(-1, shard, width).transpose(1, 0, 2).reshape(shard, -1)

    tall = ratio * shard
    attn = [attn[i * shard : i * shard + shard] for i in range(12)] + [
        attn[12 * shard],
        attn[12 * shard + 1],
    ]
    line, line_attn = attn[12:]
    grad_out_weight = jnp.concatenate(attn[:3], axis=1)
    grad_qkv = jnp.concatenate([attn[3 + 3 * g + s] for s in range(3) for g in range(3)], axis=1)

    def piece(line, i):
        return line[i * shard : i * shard + shard]

    return (
        output, grad_tokens, grad_qkv, grad_out_weight,
        wide_of(mlp[tall:]), mlp[:tall],
        piece(line_attn, 0), piece(line_attn, 1), piece(line, 5), piece(line, 3), piece(line, 4),
        line[6 * shard : 6 * shard + tall], piece(line, 2), piece(line, 0), piece(line, 1),
    )


def solution(mesh):
    rows, vector = P("dp", None), P("dp")
    return jax.shard_map(
        body, mesh=mesh, in_specs=(rows,) * 7 + (vector,) * 9, out_specs=(rows,) * 6 + (vector,) * 9,
        check_vma=False,
    )
```
